128 devices in a mesh: cluster: 8 (over y, z_hi), col: 2 (over core), blk: 8 (over z_lo, x).
Axes of the slice: x: 4, y: 4, z: 4 (z_hi: 2, z_lo: 2; z = z_hi * 2 + z_lo), core: 2. Of those that a mesh axis runs over, the one named last changes fastest.
Arguments:
- embeddings: bfloat16 [49152, 512], P(('cluster', 'col', 'blk')), may hold values from -6 to 6
- assignment: int32 [49152, 1], P(('cluster', 'col', 'blk')), may hold values from 0 to 7; in each aligned block of 384 rows (0 to 383, 384 to 767, ...) at most 128 rows name the same one
Outputs:
- best_similarity: float32 [49152], P(('cluster', 'col', 'blk'))
The draws below stay inside these ranges and needn't reach their ends.
Inputs may be any that keep to these rules, and one draw needn't show every extreme that they name: `assignment`: within the rows of one device no cluster is named more than 128 times; some cluster is named exactly 128 times in some or all devices, and every cluster is named by two or more rows in all.
All inputs are finite; a program needn't handle non-finite values.
Results may differ from the reference program's by a relative error of at most 0.0012.
Values may be sent and summed in bfloat16 or wider, within the bound.
A program may use at most 64 MiB of HBM per device.

```python
import math
import jax
import jax.numpy as jnp
import numpy as np
from jax import lax

D = 512
R_DEV = 384
CAP = 128
NCLUST = 8
ROWS = 49152


def levels(key, shape, split, low, largest):
    level = 1.0
    for axis_at, blocks in split:
        heights = jax.random.uniform(jax.random.fold_in(jax.random.fold_in(key, 6), axis_at), (blocks,), jnp.float32, low / len(split), largest / len(split))
        level = level * jnp.repeat(jnp.exp(heights), shape[axis_at] // blocks).reshape((-1,) + (1,) * (len(shape) - 1 - axis_at))
    return level


def deal_out(rng, own, number, rows, number_of, top, bound, slope):
    ranking = jax.random.permutation(rng, number_of)
    packed, usual = portions_of(number_of, rows * top, bound, slope, True), portions_of(number_of, rows * top, bound, slope, False)
    places = jnp.arange(number_of)

    def named(sizes, rotation):
        used = int((sizes > 0).sum())
        fixed = max(1, used // 4)
        passed = fixed + (places - fixed + rotation * (used - fixed)) % max(1, number_of - fixed)
        return jnp.zeros((number_of,), jnp.int32).at[ranking[jnp.where(places < fixed, places, passed)]].set(jnp.asarray(sizes, jnp.int32))

    sizes = jnp.where(number % 4 == 0, named(packed, number // 4), named(usual, number - number // 4 - 1))
    mixed = jax.random.permutation(jax.random.fold_in(own, 3), number_of)
    donor, taker = mixed[0:number_of // 2 * 2:2], mixed[1:number_of // 2 * 2:2]
    room = jnp.minimum(sizes[donor] - 1, bound - sizes[taker]) // 2
    room = jnp.where((donor == ranking[0]) | (taker == ranking[0]) | (sizes[taker] == 0), 0, jnp.maximum(room, 0))
    passed = jax.random.randint(jax.random.fold_in(own, 4), (number_of // 2,), 0, 1 << 20) % (room + 1)
    sizes = sizes.at[donor].add(-passed).at[taker].add(passed)
    members = jnp.searchsorted(jnp.cumsum(sizes), jnp.arange(rows * top), side="right").astype(jnp.int32)
    table = members.reshape(top, rows).T
    table = table[jax.random.permutation(jax.random.fold_in(own, 1), rows)]
    rotation = jax.random.randint(jax.random.fold_in(own, 2), (rows, 1), 0, top)
    return jnp.take_along_axis(table, (jnp.arange(top)[None, :] + rotation) % top, axis=1)


def portions_of(number_of, total, limit, lean, full):
    portions = [(1 << 20) // math.isqrt(grade ** lean) + 1 for grade in range(1, number_of + 1)]
    largest = limit if full else min(limit, max(-(-total // number_of), total * portions[0] // sum(portions)))
    least = 1 if total - largest >= number_of - 1 else 0
    holding, spare = [largest] + [least] * (number_of - 1), total - largest - least * (number_of - 1)
    while spare > 0:
        candidates = [i for i in range(1, number_of) if holding[i] < largest] or [i for i in range(1, number_of) if holding[i] < limit]
        pool, left = sum([portions[i] for i in candidates]), spare
        for i in candidates:
            addition = min(limit - holding[i], max(1, left * portions[i] // pool), spare)
            holding[i] = holding[i] + addition
            spare = spare - addition
    return np.array(holding)


def scatter_about(stream_key, shape, deviation, most, split=(), kind=jnp.bfloat16):
    array = deviation * jax.random.normal(stream_key, shape, jnp.float32)
    if split:
        array = array * levels(stream_key, shape, split, -0.22, 0.18)
    return jnp.clip(array, -most, most).astype(kind)


def setup_inputs(seed: int = 0) -> dict:
    streams_of = jax.random.split(jax.random.key(seed), 3)
    embeddings = scatter_about(streams_of[0], (ROWS, D), 1.0, 6.0, ((0, 128),))
    assignment_keys = jax.random.split(jax.random.fold_in(streams_of[1], 1), ROWS // R_DEV)
    assignment_turns = jax.random.permutation(jax.random.fold_in(streams_of[1], 3), ROWS // R_DEV)
    assignment = jax.vmap(lambda own, number: deal_out(jax.random.fold_in(streams_of[1], 2), own, number, R_DEV, NCLUST, 1, CAP, 2))(assignment_keys, assignment_turns).reshape((ROWS, 1))
    return {"embeddings": embeddings, "assignment": assignment}


def normalize(embeddings):
    values = embeddings.astype(jnp.float32)
    scaled = values * lax.rsqrt(lax.optimization_barrier(jnp.mean(values * values, axis=-1, keepdims=True)) + 1e-06) / math.sqrt(D)
    return scaled.astype(jnp.bfloat16)

def reference(embeddings, assignment):
    unit_rows = normalize(embeddings)
    cluster_ids = assignment[:, 0]
    row_numbers = jnp.arange(ROWS, dtype=jnp.int32)
    block_count = ROWS // R_DEV

    def one_block(block_args):
        row_piece, piece_clusters, piece_numbers = block_args
        scores = jnp.dot(row_piece, unit_rows.T, preferred_element_type=jnp.float32)
        allowed = (piece_clusters[:, None] == cluster_ids[None, :]) & (piece_numbers[:, None] != row_numbers[None, :])
        return lax.optimization_barrier(jnp.max(jnp.where(allowed, scores, -jnp.inf), axis=1))
    blocks = (unit_rows.reshape(block_count, R_DEV, D), cluster_ids.reshape(block_count, R_DEV), row_numbers.reshape(block_count, R_DEV))
    return lax.map(one_block, blocks).reshape(ROWS)
```

```python
import jax
import jax.numpy as jnp
from jax import lax
from jax.experimental import pallas as pl
from jax.experimental.pallas import tpu as pltpu
from jax.sharding import PartitionSpec as P

MESH = pl.DeviceIdType.MESH
NT = (((1,), (1,)), ((), ()))
NEG = float("-inf")
PIECES = 3
PIECE = 128
DIRECTIONS = [(1, 0, 0), (-1, 0, 0), (0, 1, 0), (0, -1, 0), (0, 0, 1), (0, 0, -1)]
TWIST = 1
SLOTS = [
    (0, 0, 0), (0, 0, 1), (0, 0, 3), (0, 1, 0), (0, 1, 1), (0, 2, 0), (0, 2, 1), (1, 0, 3), (2, 0, 0), (2, 0, 3),
    (3, 0, 0), (3, 0, 3), (3, 3, 0),
]
SENDS = [
    (0, 1, 1, 5), (0, 2, 0, 4), (0, 3, 1, 3), (0, 10, 1, 0), (0, 2, 1, 4), (0, 10, 0, 0), (0, 1, 2, 5), (0, 3, 2,
    3), (10, 12, 1, 2), (2, 7, 0, 1), (3, 5, 1, 3), (3, 11, 1, 4), (2, 11, 0, 0), (10, 4, 1, 5), (10, 12, 0, 2), (2,
    7, 1, 1), (10, 8, 0, 0), (10, 4, 0, 5), (3, 11, 2, 4), (3, 5, 2, 3), (7, 9, 0, 1), (11, 3, 0, 5), (0, 2, 2, 4),
    (0, 10, 2, 0), (1, 4, 2, 3), (7, 9, 1, 1), (4, 1, 0, 2), (8, 6, 0, 5), (5, 9, 2, 4), (10, 8, 1, 0), (4, 6, 1,
    3), (10, 12, 2, 2), (2, 7, 2, 1), (10, 8, 2, 0), (9, 5, 0, 5), (4, 6, 2, 3),
]
STEPS = [
    (0, 0, []),
    (0, 1, []),
    (0, 2, []),
    (1, 1, [(0, 0), (0, 1), (0, 2)]),
    (2, 0, [(0, 0), (0, 2), (1, 1)]),
    (3, 1, [(0, 0), (0, 1), (0, 2), (1, 1), (2, 0)]),
    (10, 1, [(0, 0), (0, 1), (0, 2), (1, 1), (2, 0), (3, 1)]),
    (1, 2, [(0, 1), (0, 2), (2, 0), (3, 1), (10, 1)]),
    (2, 1, [(0, 0), (1, 1), (1, 2), (3, 1), (10, 1)]),
    (3, 2, [(0, 0), (0, 1), (0, 2), (1, 1), (1, 2), (2, 0), (2, 1), (10, 1)]),
    (10, 0, [(0, 0), (0, 1), (0, 2), (1, 1), (1, 2), (2, 0), (2, 1), (3, 1), (3, 2)]),
    (7, 0, [(0, 2), (1, 1), (1, 2), (2, 0), (3, 1), (3, 2), (10, 0), (10, 1)]),
    (12, 1, [(0, 0), (1, 1), (1, 2), (2, 0), (3, 1), (3, 2), (7, 0), (10, 0)]),
    (4, 1, [(0, 2), (2, 0), (2, 1), (7, 0), (12, 1)]),
    (5, 1, [(0, 0), (0, 1), (0, 2), (1, 1), (1, 2), (2, 0), (2, 1), (7, 0), (10, 0), (12, 1)]),
    (11, 0, [(0, 0), (0, 1), (0, 2), (1, 1), (1, 2), (3, 1), (3, 2), (4, 1), (5, 1), (7, 0)]),
    (11, 1, [(0, 0), (1, 1), (1, 2), (3, 1), (3, 2), (4, 1), (5, 1)]),
    (7, 1, [(0, 2), (1, 2), (3, 1), (3, 2), (4, 1), (5, 1), (10, 0)]),
    (12, 0, [(0, 0), (1, 2), (2, 0), (2, 1), (3, 2), (5, 1), (7, 0), (7, 1), (11, 0), (11, 1)]),
    (4, 0, [(0, 2), (2, 0), (2, 1), (3, 2), (7, 0), (7, 1), (11, 0), (11, 1)]),
    (5, 2, [(0, 0), (0, 2), (1, 1), (1, 2), (2, 0), (2, 1), (4, 0), (7, 0), (7, 1), (11, 0), (11, 1), (12, 0), (12, 1)]),
    (8, 0, [(0, 0), (0, 1), (0, 2), (3, 1), (3, 2), (4, 0), (5, 1), (5, 2), (12, 0)]),
    (11, 2, [(1, 2), (3, 1), (3, 2), (4, 0), (4, 1), (5, 1), (5, 2), (12, 0), (12, 1)]),
    (9, 0, [(0, 2), (1, 1), (1, 2), (3, 1), (3, 2), (4, 0), (4, 1), (5, 1), (5, 2), (11, 2), (12, 0), (12, 1)]),
    (2, 2, [(1, 2), (3, 1), (3, 2), (4, 0), (4, 1), (5, 1), (5, 2), (8, 0), (12, 0), (12, 1)]),
    (3, 0, [(2, 0), (2, 1), (2, 2), (7, 0), (7, 1), (8, 0), (9, 0), (11, 0), (11, 1), (11, 2), (12, 0), (12, 1)]),
    (4, 2, [(0, 2), (1, 1), (1, 2), (2, 0), (2, 1), (2, 2), (7, 0), (7, 1), (9, 0), (11, 0), (11, 1), (11, 2), (12, 0), (12, 1)]),
    (10, 2, [(0, 0), (1, 2), (3, 0), (3, 1), (3, 2), (4, 2), (5, 1), (5, 2)]),
    (1, 0, [(2, 0), (7, 0), (8, 0), (9, 0)]),
    (9, 1, [(1, 1), (1, 2), (3, 0), (3, 1), (3, 2), (4, 0), (4, 1), (4, 2), (5, 1), (5, 2), (12, 0), (12, 1)]),
    (6, 0, [(2, 0), (2, 1), (2, 2), (7, 0), (7, 1), (8, 0), (9, 0), (9, 1), (10, 2), (11, 1), (11, 2)]),
    (6, 1, [(1, 1), (1, 2), (2, 1), (2, 2), (9, 1), (10, 2), (11, 1), (11, 2)]),
    (8, 1, [(1, 0), (3, 0), (3, 1), (3, 2), (4, 0), (5, 1), (5, 2), (6, 0), (12, 0)]),
    (9, 2, [(1, 2), (3, 0), (3, 1), (3, 2), (4, 0), (4, 1), (4, 2), (5, 1), (5, 2), (6, 0), (6, 1), (12, 0), (12, 1)]),
    (7, 2, [(3, 0), (3, 1), (3, 2), (4, 0), (4, 1), (4, 2), (5, 1), (5, 2), (6, 0), (6, 1)]),
    (12, 2, [(3, 0), (4, 2), (5, 1), (5, 2), (9, 0), (9, 1), (9, 2)]),
    (5, 0, [(2, 2), (7, 2), (8, 0), (9, 2), (11, 0), (11, 1), (11, 2), (12, 2)]),
    (6, 2, [(1, 2), (2, 2), (9, 2), (11, 2)]),
    (8, 2, [(3, 0), (3, 1), (3, 2), (5, 2)]),
]
ORDER = [
    (1, 0), (1, 1), (1, 2), (1, 3), (2, 0), (2, 1), (2, 2), (1, 4), (1, 5), (1, 6), (1, 7), (0, 0), (0, 1), (0, 2),
    (0, 3), (1, 8), (1, 9), (1, 10), (1, 11), (1, 12), (1, 13), (2, 3), (2, 4), (2, 5), (2, 6), (0, 4), (0, 5), (0,
    6), (0, 7), (1, 14), (1, 15), (1, 16), (1, 17), (1, 18), (1, 19), (2, 7), (2, 8), (2, 9), (2, 10), (0, 8), (0,
    9), (1, 20), (0, 10), (0, 11), (0, 12), (0, 13), (2, 11), (1, 21), (1, 22), (1, 23), (1, 24), (2, 12), (2, 13),
    (2, 14), (2, 15), (0, 14), (0, 15), (2, 16), (0, 16), (0, 17), (0, 18), (0, 19), (1, 25), (1, 26), (2, 17), (1,
    27), (1, 28), (1, 29), (1, 30), (2, 18), (2, 19), (2, 20), (2, 21), (0, 20), (2, 22), (0, 21), (0, 22), (0, 23),
    (0, 24), (1, 31), (1, 32), (2, 23), (1, 33), (1, 34), (1, 35), (2, 24), (2, 25), (2, 26), (0, 25), (0, 26), (2,
    27), (3, 0), (0, 27), (0, 28), (0, 29), (0, 30), (2, 28), (2, 29), (2, 30), (2, 31), (3, 10), (2, 32), (0, 31),
    (0, 32), (2, 33), (0, 33), (0, 34), (0, 35), (2, 34), (2, 35), (3, 4), (2, 36), (3, 7), (3, 12), (2, 37), (3,
    1), (3, 2), (3, 11), (3, 9), (3, 6), (2, 38), (3, 3), (3, 5), (3, 8),
]


def device_at(offset, core):
    cluster = lax.axis_index("cluster")
    blk = lax.axis_index("blk")
    x, y, z = blk % 4, cluster // 2, (cluster % 2) * 2 + blk // 4
    odd = z % 2
    dx, dy, dz = offset
    if TWIST == 1:
        dx, dy = dx - odd * (dx + dy), dy - odd * (dx + dy)
    elif TWIST == 2:
        dx, dy = dx + odd * (dy - dx), dy + odd * (dx - dy)
    elif TWIST == 3:
        dx, dy = dx - odd * (2 * dx), dy - odd * (2 * dy)
    elif TWIST == 4:
        dx = dx - odd * (2 * dx)
    x, y, z = (x + dx + 8) % 4, (y + dy + 8) % 4, (z + dz + 8) % 4
    return (y * 2 + z // 2, core, (z % 2) * 4 + x)


def kernel(
    x_ref, id_ref, o_ref, x_in, id_in, rows, ids, id_rows, row_best, col_best, partial, returned,
    load_sem, send_sem, recv_sem, id_send, id_recv, twin_send, twin_recv, twin_id_send, twin_id_recv,
    home_send, home_recv,
):
    core = lax.axis_index("col")
    twin = 1 - core
    here = (0, 0, 0)
    slots = len(SLOTS)

    barrier = pltpu.get_barrier_semaphore()
    for direction in DIRECTIONS:
        pl.semaphore_signal(barrier, inc=1, device_id=device_at(direction, core), device_id_type=MESH)
    pl.semaphore_signal(barrier, inc=1, device_id=device_at(here, twin), device_id_type=MESH)
    load = pltpu.make_async_copy(x_ref, x_in, load_sem.at[0])
    load_ids = pltpu.make_async_copy(id_ref, id_in, load_sem.at[1])
    load.start()
    load_ids.start()

    def remote(src, dst, send, recv, device):
        return pltpu.make_async_remote_copy(
            src_ref=src, dst_ref=dst, send_sem=send, recv_sem=recv, device_id=device, device_id_type=MESH
        )

    def spread_ids(slot):
        for piece in range(PIECES):
            lane_ids = ids[slot, core, :, piece * PIECE:(piece + 1) * PIECE]
            id_rows[slot, piece] = jnp.broadcast_to(lane_ids, (PIECE, PIECE)).T

    started = []

    def start(copy):
        copy.start()
        started.append(copy)

    def to_twin(slot, piece):
        copy = remote(
            rows.at[slot, piece, core], rows.at[slot, piece, core],
            twin_send.at[slot, piece], twin_recv.at[slot, piece], device_at(here, twin),
        )
        start(copy)

    def ids_to_twin(slot):
        copy = remote(
            ids.at[slot, core], ids.at[slot, core], twin_id_send.at[slot], twin_id_recv.at[slot],
            device_at(here, twin),
        )
        start(copy)

    def twin_wait(slot, piece):
        remote(
            rows.at[slot, piece, twin], rows.at[slot, piece, twin],
            twin_send.at[slot, piece], twin_recv.at[slot, piece], device_at(here, twin),
        ).wait_recv()

    def twin_ids_wait(slot):
        remote(
            ids.at[slot, twin], ids.at[slot, twin], twin_id_send.at[slot], twin_id_recv.at[slot],
            device_at(here, twin),
        ).wait_recv()

    load_ids.wait()
    ids[0, core] = id_in[...].astype(jnp.float32)
    load.wait()
    features = x_in.shape[1]
    for piece in range(PIECES):
        values = x_in[piece * PIECE:(piece + 1) * PIECE].astype(jnp.float32)
        mean = jnp.mean(values * values, axis=-1, keepdims=True)
        scale = lax.rsqrt(mean + 1e-06) * (1.0 / features**0.5)
        rows[0, piece, core] = (values * scale).astype(jnp.bfloat16)
    pl.semaphore_wait(barrier, len(DIRECTIONS) + 1)

    id_fresh, twin_id_fresh = set(), set()
    row_touched, col_touched = set(), set()

    def piece_copy(index):
        src, dst, piece, direction = SENDS[index]
        return remote(
            rows.at[src, piece, core], rows.at[dst, piece, core],
            send_sem.at[index], recv_sem.at[dst, piece], device_at(DIRECTIONS[direction], core),
        )

    def id_copy(index):
        src, dst, piece, direction = SENDS[index]
        return remote(
            ids.at[src, core], ids.at[dst, core], id_send.at[dst], id_recv.at[dst],
            device_at(DIRECTIONS[direction], core),
        )

    first_for = {}
    for index, (src, dst, piece, direction) in enumerate(SENDS):
        first_for.setdefault(dst, index)

    def arrive(index):
        src, dst, piece, direction = SENDS[index]
        if first_for[dst] == index:
            id_copy(index).wait_recv()
            ids_to_twin(dst)
        piece_copy(index).wait_recv()
        to_twin(dst, piece)
        if first_for[dst] == index:
            spread_ids(dst)

    def send(index):
        src, dst, piece, direction = SENDS[index]
        start(piece_copy(index))
        if first_for[dst] == index:
            start(id_copy(index))

    def step(index):
        slot, piece, others = STEPS[index]
        if slot not in twin_id_fresh:
            twin_id_fresh.add(slot)
            twin_ids_wait(slot)
        twin_wait(slot, piece)
        own = [(0, p) for p in range(PIECES)] if slot == 0 else []
        left = others + own
        columns = rows[slot, piece].reshape(2 * PIECE, features)
        stacked = jnp.concatenate([rows[s, p, core] for s, p in left], axis=0)
        scores = lax.dot_general(stacked, columns, NT, preferred_element_type=jnp.float32)
        for half in range(2):
            lane_ids = ids[slot, half, :, piece * PIECE:(piece + 1) * PIECE]
            columns_best = None
            for at, (s, p) in enumerate(left):
                block = scores[at * PIECE:(at + 1) * PIECE, half * PIECE:(half + 1) * PIECE]
                allowed = id_rows[s, p] == lane_ids
                if (s, p) in own and p == piece:
                    r = lax.broadcasted_iota(jnp.int32, (PIECE, PIECE), 0)
                    c = lax.broadcasted_iota(jnp.int32, (PIECE, PIECE), 1)
                    allowed = allowed & (r + PIECE * core != c + PIECE * half)
                block = jnp.where(allowed, block, NEG)
                if (s, p) in row_touched:
                    row_best[s, p] = jnp.maximum(row_best[s, p], block)
                else:
                    row_best[s, p] = block
                    row_touched.add((s, p))
                if slot != 0:
                    best = jnp.max(block.reshape(PIECE // 8, 8, PIECE), axis=0)
                    columns_best = best if columns_best is None else jnp.maximum(columns_best, best)
            if columns_best is not None:
                col_best[slot, piece, half] = columns_best
                col_touched.add((slot, piece))

    def home_copy(slot, to_core):
        if slot == 0:
            return remote(
                partial.at[0, twin], returned.at[0, core], home_send.at[0, 0], home_recv.at[0, core],
                device_at(here, twin),
            )
        return remote(
            partial.at[slot, to_core], returned.at[slot, core], home_send.at[slot, to_core],
            home_recv.at[slot, core], device_at(SLOTS[slot], to_core),
        )

    def go_home(slot):
        for piece in range(PIECES):
            mine = None
            if (slot, piece) in row_touched:
                mine = jnp.max(row_best[slot, piece].T, axis=0, keepdims=True)
            for half in range(2):
                best = jnp.full((1, PIECE), NEG, jnp.float32)
                if mine is not None:
                    best = jnp.where(core == half, mine, best)
                if (slot, piece) in col_touched:
                    best = jnp.maximum(best, jnp.max(col_best[slot, piece, half], axis=0, keepdims=True))
                partial[slot, half, :, piece * PIECE:(piece + 1) * PIECE] = best
        if slot == 0:
            start(home_copy(0, None))
        else:
            for to_core in range(2):
                start(home_copy(slot, to_core))

    for piece in range(PIECES):
        to_twin(0, piece)
    ids_to_twin(0)
    spread = False
    for kind, index in ORDER:
        if kind == 2 and not spread:
            spread = True
            spread_ids(0)
        (arrive, send, step, go_home)[kind](index)

    best = partial[0, core]
    remote(
        partial.at[0, core], returned.at[0, twin], home_send.at[0, 0], home_recv.at[0, twin], device_at(here, twin)
    ).wait_recv()
    best = jnp.maximum(best, returned[0, twin])
    for slot in range(1, slots):
        for half in range(2):
            remote(
                partial.at[slot, half], returned.at[slot, half], home_send.at[slot, half],
                home_recv.at[slot, half], device_at(here, twin),
            ).wait_recv()
            best = jnp.maximum(best, returned[slot, half])
    o_ref[...] = best
    for copy in started:
        copy.wait_send()


def local(embeddings, assignment):
    count, features = embeddings.shape
    slots = len(SLOTS)
    dma = pltpu.SemaphoreType.DMA
    best = pl.pallas_call(
        kernel,
        out_shape=jax.ShapeDtypeStruct((1, count), jnp.float32),
        in_specs=[pl.BlockSpec(memory_space=pl.ANY)] * 2,
        out_specs=pl.BlockSpec(memory_space=pltpu.VMEM),
        scratch_shapes=[
            pltpu.VMEM((count, features), jnp.bfloat16),
            pltpu.VMEM((1, count), jnp.int32),
            pltpu.VMEM((slots, PIECES, 2, PIECE, features), jnp.bfloat16),
            pltpu.VMEM((slots, 2, 1, count), jnp.float32),
            pltpu.VMEM((slots, PIECES, PIECE, PIECE), jnp.float32),
            pltpu.VMEM((slots, PIECES, PIECE, PIECE), jnp.float32),
            pltpu.VMEM((slots, PIECES, 2, 8, PIECE), jnp.float32),
            pltpu.VMEM((slots, 2, 1, count), jnp.float32),
            pltpu.VMEM((slots, 2, 1, count), jnp.float32),
            dma((2,)),
            dma((len(SENDS),)),
            dma((slots, PIECES)),
            dma((slots,)),
            dma((slots,)),
            dma((slots, PIECES)),
            dma((slots, PIECES)),
            dma((slots,)),
            dma((slots,)),
            dma((slots, 2)),
            dma((slots, 2)),
        ],
        compiler_params=pltpu.CompilerParams(
            collective_id=0, has_side_effects=True, vmem_limit_bytes=56 * 2**20
        ),
    )(embeddings, assignment.reshape(1, count))
    return best.reshape(count)


def solution(mesh):
    axes = ("cluster", "col", "blk")
    return jax.shard_map(
        local, mesh=mesh, in_specs=(P(axes, None), P(axes, None)), out_specs=P(axes), check_vma=False
    )
```

```python
import jax
import jax.numpy as jnp
from jax import lax
from jax.experimental import pallas as pl
from jax.experimental.pallas import tpu as pltpu
from jax.sharding import PartitionSpec as P

MESH = pl.DeviceIdType.MESH
NT = (((1,), (1,)), ((), ()))
NEG = float("-inf")
PIECES = 3
PIECE = 128
DIRECTIONS = [(1, 0, 0), (-1, 0, 0), (0, 1, 0), (0, -1, 0), (0, 0, 1), (0, 0, -1)]
TWIST = 4
SLOTS = [
    (0, 0, 0), (0, 0, 1), (0, 0, 3), (0, 1, 0), (0, 1, 3), (0, 2, 0), (0, 2, 3), (0, 3, 0), (1, 0, 0), (1, 0, 1),
    (2, 0, 0), (2, 0, 1), (3, 0, 1), (3, 0, 2),
]
SENDS = [
    (0, 8, 1, 1), (0, 7, 2, 2), (0, 3, 1, 3), (0, 2, 2, 4), (0, 1, 0, 5), (0, 8, 0, 1), (0, 7, 0, 2), (0, 3, 0, 3),
    (0, 2, 0, 4), (0, 1, 2, 5), (0, 8, 2, 1), (0, 7, 1, 2), (0, 3, 2, 3), (0, 2, 1, 4), (0, 1, 1, 5), (1, 12, 0, 0),
    (8, 10, 1, 1), (7, 5, 2, 2), (2, 4, 2, 3), (3, 4, 1, 4), (8, 12, 1, 5), (1, 12, 2, 0), (1, 9, 2, 1), (7, 5, 0,
    2), (2, 4, 0, 3), (12, 11, 0, 0), (8, 10, 0, 1), (7, 5, 1, 2), (10, 11, 1, 5), (5, 6, 2, 4), (4, 6, 1, 3), (8,
    10, 2, 1), (12, 11, 2, 0), (9, 13, 2, 5), (5, 6, 0, 4), (11, 9, 0, 0), (1, 9, 1, 1),
]
STEPS = [
    (0, 0, []),
    (0, 1, []),
    (0, 2, []),
    (8, 1, [(0, 0), (0, 1), (0, 2), (1, 0), (2, 2), (3, 1), (7, 2)]),
    (7, 2, [(0, 0), (0, 1), (0, 2), (1, 0), (2, 2), (3, 1)]),
    (2, 2, [(0, 0), (0, 1), (0, 2), (1, 0), (3, 1)]),
    (3, 1, [(0, 0), (0, 1), (1, 0)]),
    (1, 0, [(0, 0), (0, 1)]),
    (8, 0, [(0, 0), (0, 1), (0, 2), (1, 0), (1, 2), (2, 2), (3, 0), (3, 1), (7, 0), (7, 2)]),
    (7, 0, [(0, 0), (0, 2), (1, 0), (1, 2), (2, 0), (2, 2), (3, 0), (3, 1), (8, 1)]),
    (1, 2, [(0, 0), (0, 1), (2, 2), (3, 0), (3, 1), (7, 2), (8, 1)]),
    (2, 0, [(0, 1), (1, 0), (3, 1), (8, 1)]),
    (3, 0, [(0, 1), (1, 1), (2, 1), (7, 2), (8, 1), (8, 2), (12, 0)]),
    (8, 2, [(0, 0), (0, 1), (0, 2), (1, 2), (3, 1), (3, 2), (7, 0), (7, 1), (7, 2), (12, 0)]),
    (7, 1, [(0, 2), (1, 1), (1, 2), (2, 1), (2, 2), (3, 1), (8, 0), (8, 1), (12, 0)]),
    (12, 0, [(2, 0), (2, 1), (2, 2), (3, 1), (3, 2), (7, 0), (7, 2), (8, 0), (8, 1)]),
    (2, 1, [(0, 1), (1, 0), (1, 1), (1, 2), (5, 2), (8, 1), (10, 1), (12, 1), (12, 2)]),
    (3, 2, [(7, 2), (8, 0), (8, 1), (10, 1), (12, 1), (12, 2)]),
    (1, 1, [(4, 1), (4, 2), (5, 2)]),
    (10, 1, [(0, 0), (0, 1), (0, 2), (1, 2), (2, 0), (2, 2), (3, 0), (3, 1), (4, 1), (4, 2), (5, 2), (7, 0), (7, 2), (12, 0), (12, 1), (12, 2)]),
    (5, 2, [(1, 0), (1, 2), (2, 0), (8, 0), (8, 1), (8, 2), (9, 2), (11, 0), (12, 0), (12, 1), (12, 2)]),
    (12, 2, [(2, 0), (2, 2), (3, 0), (3, 1), (4, 0), (4, 1), (4, 2), (5, 0), (7, 0), (7, 1), (7, 2), (8, 0), (8, 2), (9, 2)]),
    (12, 1, [(2, 0), (2, 2), (3, 0), (3, 1), (4, 0), (4, 1), (4, 2), (5, 0), (7, 0), (7, 1), (7, 2)]),
    (4, 1, [(1, 0), (1, 2), (7, 0), (7, 1), (9, 2), (10, 0), (11, 0), (11, 1), (12, 0)]),
    (4, 2, [(1, 0), (1, 2), (9, 2), (10, 0), (11, 0), (11, 1), (11, 2), (12, 0)]),
    (9, 2, [(0, 0), (0, 2), (3, 0), (3, 1), (3, 2), (4, 0), (5, 0), (5, 1), (6, 1), (6, 2), (7, 0), (7, 1), (7, 2), (12, 0)]),
    (11, 0, [(1, 0), (2, 0), (2, 1), (2, 2), (3, 0), (4, 0), (5, 0), (5, 1), (6, 1), (6, 2), (7, 0), (7, 1), (7, 2), (8, 0), (8, 2)]),
    (5, 0, [(1, 0), (1, 1), (8, 0), (8, 1), (8, 2), (10, 0), (10, 1), (10, 2), (11, 1), (11, 2), (12, 0), (13, 2)]),
    (4, 0, [(1, 0), (1, 1), (1, 2), (9, 0), (10, 1), (10, 2), (11, 1), (11, 2), (12, 0), (13, 2)]),
    (6, 1, [(1, 0), (1, 1), (1, 2), (8, 0), (8, 1), (8, 2), (9, 0), (10, 1), (10, 2), (11, 1), (11, 2), (12, 0), (12, 1), (12, 2), (13, 2)]),
    (11, 1, [(2, 1), (2, 2), (5, 2), (7, 0), (7, 1), (7, 2), (8, 0), (8, 2)]),
    (5, 1, [(8, 0), (8, 1), (8, 2), (9, 0), (9, 1), (10, 1)]),
    (10, 0, [(3, 0), (3, 2), (7, 2)]),
    (6, 2, [(1, 0), (1, 2), (9, 0), (10, 2), (11, 2)]),
    (11, 2, [(2, 2), (3, 1), (3, 2), (4, 1), (7, 0), (7, 1), (7, 2)]),
    (6, 0, [(1, 0), (9, 0), (11, 0), (13, 2)]),
    (10, 2, [(3, 2), (5, 2)]),
    (9, 0, [(3, 0), (3, 1), (3, 2), (4, 1), (4, 2), (5, 0), (7, 0), (7, 1)]),
    (9, 1, [(3, 0), (3, 1), (3, 2), (4, 0), (4, 1), (4, 2), (5, 0), (7, 0), (7, 1), (7, 2)]),
]
ORDER = [
    (1, 0), (1, 1), (1, 2), (1, 3), (1, 4), (1, 5), (1, 6), (1, 7), (1, 8), (1, 9), (2, [0, 1, 2]), (1, 10), (1,
    11), (1, 12), (1, 13), (1, 14), (0, 0), (0, 1), (0, 2), (0, 3), (0, 4), (1, 15), (1, 16), (1, 17), (1, 18), (1,
    19), (1, 20), (2, [3, 4, 5]), (2, [6, 7]), (0, 5), (0, 6), (0, 7), (0, 8), (0, 9), (1, 21), (1, 22), (1, 23),
    (1, 24), (2, [8, 9, 10]), (2, [11]), (0, 10), (0, 11), (0, 12), (0, 13), (0, 14), (0, 15), (1, 25), (1, 26), (1,
    27), (2, [12, 13, 14]), (2, [15]), (0, 16), (1, 28), (0, 17), (1, 29), (0, 18), (0, 19), (1, 30), (0, 20), (1,
    31), (0, 21), (1, 32), (2, [16, 17, 18]), (2, [19]), (0, 22), (1, 33), (0, 23), (1, 34), (0, 24), (0, 25), (1,
    35), (1, 36), (2, [20, 21, 22]), (0, 26), (0, 28), (0, 27), (0, 29), (0, 30), (2, [23]), (0, 32), (2, [24, 25]),
    (3, [0]), (2, [26]), (0, 31), (0, 33), (0, 34), (2, [27]), (0, 35), (2, [28, 29]), (3, [12]), (0, 36), (2, [30,
    31]), (3, [8]), (2, [32, 33, 34]), (3, [2]), (2, [35]), (3, [11, 6, 13, 1]), (2, [36]), (3, [10]), (2, [37,
    38]), (3, [5, 4, 9, 3, 7]),
]


def device_at(offset, core):
    cluster = lax.axis_index("cluster")
    blk = lax.axis_index("blk")
    x, y, z = blk % 4, cluster // 2, (cluster % 2) * 2 + blk // 4
    odd = z % 2
    dx, dy, dz = offset
    if TWIST == 1:
        dx, dy = dx - odd * (dx + dy), dy - odd * (dx + dy)
    elif TWIST == 2:
        dx, dy = dx + odd * (dy - dx), dy + odd * (dx - dy)
    elif TWIST == 3:
        dx, dy = dx - odd * (2 * dx), dy - odd * (2 * dy)
    elif TWIST == 4:
        dx = dx - odd * (2 * dx)
    x, y, z = (x + dx + 8) % 4, (y + dy + 8) % 4, (z + dz + 8) % 4
    return (y * 2 + z // 2, core, (z % 2) * 4 + x)


def kernel(
    x_ref, id_ref, o_ref, x_in, id_in, rows, ids, id_rows, row_best, col_best, partial, returned,
    load_sem, send_sem, recv_sem, id_send, id_recv, twin_send, twin_recv, twin_id_send, twin_id_recv,
    home_send, home_recv,
):
    core = lax.axis_index("col")
    twin = 1 - core
    here = (0, 0, 0)
    slots = len(SLOTS)

    barrier = pltpu.get_barrier_semaphore()
    for direction in DIRECTIONS:
        pl.semaphore_signal(barrier, inc=1, device_id=device_at(direction, core), device_id_type=MESH)
    pl.semaphore_signal(barrier, inc=1, device_id=device_at(here, twin), device_id_type=MESH)
    load = pltpu.make_async_copy(x_ref, x_in, load_sem.at[0])
    load_ids = pltpu.make_async_copy(id_ref, id_in, load_sem.at[1])
    load.start()
    load_ids.start()

    def remote(src, dst, send, recv, device):
        return pltpu.make_async_remote_copy(
            src_ref=src, dst_ref=dst, send_sem=send, recv_sem=recv, device_id=device, device_id_type=MESH
        )

    def spread_ids(slot):
        for piece in range(PIECES):
            lane_ids = ids[slot, core, :, piece * PIECE:(piece + 1) * PIECE]
            id_rows[slot, piece] = jnp.broadcast_to(lane_ids, (PIECE, PIECE)).T

    started = []

    def start(copy):
        copy.start()
        started.append(copy)

    def to_twin(slot, piece):
        copy = remote(
            rows.at[slot, piece, core], rows.at[slot, piece, core],
            twin_send.at[slot, piece], twin_recv.at[slot, piece], device_at(here, twin),
        )
        start(copy)

    def ids_to_twin(slot):
        copy = remote(
            ids.at[slot, core], ids.at[slot, core], twin_id_send.at[slot], twin_id_recv.at[slot],
            device_at(here, twin),
        )
        start(copy)

    def twin_wait(slot, piece):
        remote(
            rows.at[slot, piece, twin], rows.at[slot, piece, twin],
            twin_send.at[slot, piece], twin_recv.at[slot, piece], device_at(here, twin),
        ).wait_recv()

    def twin_ids_wait(slot):
        remote(
            ids.at[slot, twin], ids.at[slot, twin], twin_id_send.at[slot], twin_id_recv.at[slot],
            device_at(here, twin),
        ).wait_recv()

    load_ids.wait()
    ids[0, core] = id_in[...].astype(jnp.float32)
    load.wait()
    features = x_in.shape[1]
    for piece in range(PIECES):
        values = x_in[piece * PIECE:(piece + 1) * PIECE].astype(jnp.float32)
        mean = jnp.mean(values * values, axis=-1, keepdims=True)
        scale = lax.rsqrt(mean + 1e-06) * (1.0 / features**0.5)
        rows[0, piece, core] = (values * scale).astype(jnp.bfloat16)
    pl.semaphore_wait(barrier, len(DIRECTIONS) + 1)

    id_fresh, twin_id_fresh = set(), set()
    row_touched, col_touched, spread = set(), set(), set()

    def piece_copy(index):
        src, dst, piece, direction = SENDS[index]
        return remote(
            rows.at[src, piece, core], rows.at[dst, piece, core],
            send_sem.at[index], recv_sem.at[dst, piece], device_at(DIRECTIONS[direction], core),
        )

    def id_copy(index):
        src, dst, piece, direction = SENDS[index]
        return remote(
            ids.at[src, core], ids.at[dst, core], id_send.at[dst], id_recv.at[dst],
            device_at(DIRECTIONS[direction], core),
        )

    as_columns = {(slot, piece) for slot, piece, _ in STEPS}
    first_for = {}
    for index, (src, dst, piece, direction) in enumerate(SENDS):
        first_for.setdefault(dst, index)

    def arrive(index):
        src, dst, piece, direction = SENDS[index]
        if first_for[dst] == index:
            id_copy(index).wait_recv()
            if dst in {slot for slot, _ in as_columns}:
                ids_to_twin(dst)
        piece_copy(index).wait_recv()
        if (dst, piece) in as_columns:
            to_twin(dst, piece)

    def send(index):
        src, dst, piece, direction = SENDS[index]
        start(piece_copy(index))
        if first_for[dst] == index:
            start(id_copy(index))

    def step(batch):
        for index in batch:
            slot, piece, _ = STEPS[index]
            if slot not in twin_id_fresh:
                twin_id_fresh.add(slot)
                twin_ids_wait(slot)
            twin_wait(slot, piece)

        @pl.when(core < 2)
        def _():
            for index in batch:
                compare(*STEPS[index])

    def compare(slot, piece, others):
        own = [(0, p) for p in range(PIECES)] if slot == 0 else []
        left = others + own
        for s in sorted({s for s, _ in left} - spread):
            spread.add(s)
            spread_ids(s)
        columns = rows[slot, piece].reshape(2 * PIECE, features)
        stacked = jnp.concatenate([rows[s, p, core] for s, p in left], axis=0)
        scores = lax.dot_general(stacked, columns, NT, preferred_element_type=jnp.float32)
        lane_ids = [ids[slot, half, :, piece * PIECE:(piece + 1) * PIECE] for half in range(2)]
        columns_best = [None, None]
        for at, (s, p) in enumerate(left):
            row = row_best[s, p] if (s, p) in row_touched else None
            row_touched.add((s, p))
            for half in range(2):
                block = scores[at * PIECE:(at + 1) * PIECE, half * PIECE:(half + 1) * PIECE]
                allowed = id_rows[s, p] == lane_ids[half]
                if s == slot and p == piece:
                    r = lax.broadcasted_iota(jnp.int32, (PIECE, PIECE), 0)
                    c = lax.broadcasted_iota(jnp.int32, (PIECE, PIECE), 1)
                    allowed = allowed & (r + PIECE * core != c + PIECE * half)
                block = jnp.where(allowed, block, NEG)
                row = block if row is None else jnp.maximum(row, block)
                if s != slot:
                    best = jnp.max(block.reshape(PIECE // 8, 8, PIECE), axis=0)
                    seen = columns_best[half]
                    columns_best[half] = best if seen is None else jnp.maximum(seen, best)
            row_best[s, p] = row
        if columns_best[0] is not None:
            for half in range(2):
                col_best[slot, piece, half] = columns_best[half]
            col_touched.add((slot, piece))

    def home_copy(slot, to_core):
        if slot == 0:
            return remote(
                partial.at[0, twin], returned.at[0, core], home_send.at[0, 0], home_recv.at[0, core],
                device_at(here, twin),
            )
        return remote(
            partial.at[slot, to_core], returned.at[slot, core], home_send.at[slot, to_core],
            home_recv.at[slot, core], device_at(SLOTS[slot], to_core),
        )

    def go_home(slots_done):
        @pl.when(core < 2)
        def _():
            for slot in slots_done:
                sum_up(slot)

        for slot in slots_done:
            for to_core in range(2 if slot else 1):
                start(home_copy(slot, to_core))

    def sum_up(slot):
        for piece in range(PIECES):
            mine = None
            if (slot, piece) in row_touched:
                mine = jnp.max(row_best[slot, piece].T, axis=0, keepdims=True)
            for half in range(2):
                best = jnp.full((1, PIECE), NEG, jnp.float32)
                if mine is not None:
                    best = jnp.where(core == half, mine, best)
                if (slot, piece) in col_touched:
                    best = jnp.maximum(best, jnp.max(col_best[slot, piece, half], axis=0, keepdims=True))
                partial[slot, half, :, piece * PIECE:(piece + 1) * PIECE] = best

    for piece in range(PIECES):
        to_twin(0, piece)
    ids_to_twin(0)
    for kind, index in ORDER:
        (arrive, send, step, go_home)[kind](index)

    best = partial[0, core]
    remote(
        partial.at[0, core], returned.at[0, twin], home_send.at[0, 0], home_recv.at[0, twin], device_at(here, twin)
    ).wait_recv()
    best = jnp.maximum(best, returned[0, twin])
    for slot in range(1, slots):
        for half in range(2):
            remote(
                partial.at[slot, half], returned.at[slot, half], home_send.at[slot, half],
                home_recv.at[slot, half], device_at(here, twin),
            ).wait_recv()
            best = jnp.maximum(best, returned[slot, half])
    o_ref[...] = best
    for copy in started:
        copy.wait_send()


def local(embeddings, assignment):
    count, features = embeddings.shape
    slots = len(SLOTS)
    dma = pltpu.SemaphoreType.DMA
    best = pl.pallas_call(
        kernel,
        out_shape=jax.ShapeDtypeStruct((1, count), jnp.float32),
        in_specs=[pl.BlockSpec(memory_space=pl.ANY)] * 2,
        out_specs=pl.BlockSpec(memory_space=pltpu.VMEM),
        scratch_shapes=[
            pltpu.VMEM((count, features), jnp.bfloat16),
            pltpu.VMEM((1, count), jnp.int32),
            pltpu.VMEM((slots, PIECES, 2, PIECE, features), jnp.bfloat16),
            pltpu.VMEM((slots, 2, 1, count), jnp.float32),
            pltpu.VMEM((slots, PIECES, PIECE, PIECE), jnp.float32),
            pltpu.VMEM((slots, PIECES, PIECE, PIECE), jnp.float32),
            pltpu.VMEM((slots, PIECES, 2, 8, PIECE), jnp.float32),
            pltpu.VMEM((slots, 2, 1, count), jnp.float32),
            pltpu.VMEM((slots, 2, 1, count), jnp.float32),
            dma((2,)),
            dma((len(SENDS),)),
            dma((slots, PIECES)),
            dma((slots,)),
            dma((slots,)),
            dma((slots, PIECES)),
            dma((slots, PIECES)),
            dma((slots,)),
            dma((slots,)),
            dma((slots, 2)),
            dma((slots, 2)),
        ],
        compiler_params=pltpu.CompilerParams(
            collective_id=0, has_side_effects=True, vmem_limit_bytes=56 * 2**20
        ),
    )(embeddings, assignment.reshape(1, count))
    return best.reshape(count)


def solution(mesh):
    axes = ("cluster", "col", "blk")
    return jax.shard_map(
        local, mesh=mesh, in_specs=(P(axes, None), P(axes, None)), out_specs=P(axes), check_vma=False
    )
```

```python
import jax
import jax.numpy as jnp
from jax import lax
from jax.experimental import pallas as pl
from jax.experimental.pallas import tpu as pltpu
from jax.sharding import PartitionSpec as P

MESH = pl.DeviceIdType.MESH
NT = (((1,), (1,)), ((), ()))
NEG = float("-inf")
PIECES = 3
PIECE = 128
DIRECTIONS = [(1, 0, 0), (-1, 0, 0), (0, 1, 0), (0, -1, 0), (0, 0, 1), (0, 0, -1)]
TWIST = 0
SLOTS = [
    (0, 0, 0), (0, 0, 1), (0, 0, 2), (0, 0, 3), (0, 1, 0), (0, 3, 0), (0, 3, 1), (0, 3, 2), (0, 3, 3), (1, 0, 0),
    (2, 0, 0), (2, 1, 0), (3, 0, 0), (3, 1, 0),
]
SENDS = [
    (0, 12, 1, 0), (0, 9, 0, 1), (0, 5, 0, 2), (0, 4, 2, 3), (0, 3, 2, 4), (0, 1, 1, 5), (0, 12, 0, 0), (0, 9, 2,
    1), (0, 5, 2, 2), (0, 4, 1, 3), (0, 3, 1, 4), (0, 1, 0, 5), (0, 12, 2, 0), (0, 9, 1, 1), (0, 4, 0, 3), (0, 1, 2,
    5), (5, 8, 0, 4), (3, 8, 2, 2), (4, 13, 2, 0), (9, 10, 0, 1), (1, 6, 1, 2), (12, 13, 1, 3), (3, 2, 2, 4), (1, 2,
    1, 5), (12, 10, 1, 0), (9, 10, 2, 1), (3, 8, 1, 2), (12, 13, 0, 3), (1, 2, 0, 5), (8, 7, 2, 4), (13, 11, 2, 0),
    (1, 6, 0, 2), (8, 7, 0, 4), (10, 11, 0, 3), (6, 7, 1, 5), (13, 11, 1, 0), (1, 6, 2, 2), (8, 5, 1, 5),
]
STEPS = [
    (0, 0, []),
    (0, 1, []),
    (0, 2, []),
    (12, 1, [(0, 0), (0, 1), (0, 2), (1, 1), (3, 2), (4, 2), (5, 0), (9, 0)]),
    (5, 0, [(0, 0), (0, 1), (0, 2), (1, 1), (3, 2), (4, 2), (9, 0)]),
    (9, 0, [(0, 0), (0, 2), (1, 1), (3, 2), (4, 2)]),
    (3, 2, [(0, 0), (0, 1), (0, 2), (1, 1), (4, 2)]),
    (4, 2, [(0, 1), (0, 2), (1, 1), (3, 1), (5, 2), (9, 2), (12, 0)]),
    (1, 1, [(0, 0), (0, 1), (3, 1), (4, 1), (5, 2), (12, 0)]),
    (12, 0, [(0, 1), (0, 2), (1, 0), (3, 1), (3, 2), (4, 1), (5, 0), (5, 2), (9, 0), (9, 2)]),
    (5, 2, [(0, 0), (0, 1), (1, 0), (3, 1), (3, 2), (4, 1), (9, 0), (9, 2), (12, 1)]),
    (9, 2, [(0, 2), (3, 1), (3, 2), (12, 1)]),
    (1, 0, [(0, 0), (0, 1), (3, 1), (3, 2), (4, 0), (4, 1), (5, 0), (8, 0), (8, 2), (9, 0), (12, 1)]),
    (4, 1, [(0, 1), (3, 1), (5, 0), (8, 0), (8, 2), (9, 1), (12, 1), (12, 2)]),
    (3, 1, [(0, 2), (4, 0), (12, 1), (12, 2)]),
    (8, 0, [(0, 2), (1, 1), (1, 2), (4, 0), (4, 2), (5, 2), (9, 0), (9, 1), (9, 2), (12, 0), (12, 1), (12, 2)]),
    (8, 2, [(1, 1), (1, 2), (4, 0), (4, 2), (9, 0), (9, 1), (9, 2), (12, 0), (12, 1), (12, 2)]),
    (4, 0, [(0, 1), (1, 1), (1, 2), (5, 0), (9, 1), (12, 1)]),
    (9, 1, [(0, 2), (2, 1), (2, 2), (3, 2), (4, 2), (6, 1), (12, 1), (13, 1), (13, 2)]),
    (1, 2, [(3, 2), (9, 0), (9, 2), (10, 0), (12, 0), (13, 1), (13, 2)]),
    (10, 0, [(1, 0), (1, 1), (2, 1), (2, 2), (3, 1), (3, 2), (4, 0), (4, 1), (4, 2), (5, 2), (6, 1), (8, 0), (8, 2)]),
    (13, 2, [(1, 0), (1, 1), (2, 1), (2, 2), (3, 1), (5, 0), (5, 2), (6, 1), (8, 0), (8, 2), (9, 2)]),
    (13, 1, [(1, 0), (1, 1), (2, 0), (2, 1), (2, 2), (3, 1), (5, 0), (5, 2), (6, 1), (7, 2), (8, 0), (8, 1), (8, 2), (9, 2)]),
    (6, 1, [(3, 1), (3, 2), (4, 1), (9, 0), (9, 2), (10, 1), (10, 2), (12, 0), (13, 0)]),
    (2, 2, [(9, 0), (9, 2), (10, 1), (10, 2), (12, 0), (12, 1), (13, 0)]),
    (2, 1, [(4, 0), (9, 0), (10, 1), (12, 0), (13, 0)]),
    (8, 1, [(4, 0), (4, 2), (9, 0), (9, 1), (9, 2), (10, 0), (10, 1), (10, 2), (12, 0), (13, 0), (13, 2)]),
    (7, 2, [(4, 0), (4, 1), (4, 2), (9, 0), (9, 1), (9, 2), (10, 0), (10, 1), (10, 2), (13, 0), (13, 2)]),
    (10, 1, [(1, 1), (1, 2), (3, 2), (4, 0), (6, 0), (7, 0), (7, 1), (8, 0), (8, 2)]),
    (13, 0, [(1, 0), (1, 2), (2, 0), (5, 0), (5, 2), (6, 0), (7, 0), (7, 1), (8, 0), (8, 2)]),
    (10, 2, [(0, 2), (1, 2), (6, 0), (7, 0), (7, 1), (8, 0), (8, 2)]),
    (2, 0, [(0, 0), (9, 0), (10, 0), (11, 0), (13, 2)]),
    (11, 0, [(1, 0), (1, 2), (2, 1), (5, 0), (5, 2), (6, 0), (6, 1), (7, 0), (7, 1), (7, 2), (8, 1), (8, 2)]),
    (11, 2, [(1, 2), (5, 2), (6, 1), (7, 1), (7, 2), (8, 0), (8, 1), (8, 2)]),
    (7, 0, [(4, 0), (4, 1), (9, 0), (9, 1), (9, 2), (13, 1), (13, 2)]),
    (7, 1, [(4, 1), (9, 0), (9, 1), (9, 2), (11, 1), (13, 1), (13, 2)]),
    (6, 0, [(9, 0), (9, 1), (9, 2), (13, 1), (13, 2)]),
    (11, 1, [(1, 2), (5, 0), (5, 1), (5, 2), (6, 1)]),
    (6, 2, [(9, 0), (9, 1), (9, 2), (13, 0), (13, 1), (13, 2)]),
    (5, 1, [(4, 1), (13, 0), (13, 1), (13, 2)]),
]
ORDER = [
    (1, 0),
    (1, 1),
    (1, 2),
    (1, 3),
    (1, 4),
    (1, 5),
    (1, 6),
    (1, 7),
    (1, 8),
    (1, 9),
    (1, 10),
    (1, 11),
    (2, ([0, 1, 2], [], [])),
    (1, 12),
    (1, 13),
    (1, 14),
    (1, 15),
    (0, 0),
    (0, 1),
    (0, 2),
    (1, 16),
    (0, 3),
    (0, 4),
    (1, 17),
    (0, 5),
    (1, 18),
    (1, 19),
    (1, 20),
    (1, 21),
    (1, 22),
    (1, 23),
    (2, ([3], [], [])),
    (2, ([4, 5, 6], [], [])),
    (0, 6),
    (0, 7),
    (0, 8),
    (0, 9),
    (0, 10),
    (0, 11),
    (2, ([7, 8], [], [])),
    (1, 24),
    (1, 25),
    (1, 26),
    (1, 27),
    (1, 28),
    (2, ([9, 10, 11], [], [])),
    (0, 12),
    (0, 13),
    (0, 14),
    (0, 17),
    (1, 29),
    (0, 16),
    (0, 15),
    (2, ([12, 13, 14], [], [])),
    (2, ([15, 16, 17], [], [])),
    (0, 18),
    (1, 30),
    (1, 31),
    (1, 32),
    (0, 19),
    (1, 33),
    (0, 20),
    (1, 34),
    (0, 21),
    (0, 22),
    (0, 23),
    (2, ([18, 19], [], [])),
    (2, ([20, 21], [], [])),
    (0, 24),
    (1, 35),
    (1, 36),
    (0, 25),
    (0, 26),
    (1, 37),
    (0, 27),
    (0, 29),
    (0, 28),
    (2, ([22, 23, 24], [], [])),
    (2, ([25, 26, 27], [], [])),
    (0, 30),
    (0, 31),
    (0, 32),
    (0, 33),
    (0, 34),
    (2, ([28, 29, 30], [12], [])),
    (2, ([31, 32, 33], [3], [])),
    (0, 35),
    (0, 36),
    (0, 37),
    (2, ([34, 35, 36], [10, 2, 8, 0], [])),
    (2, ([37], [7], [])),
    (2, ([38, 39], [11, 1], [6, 13, 9, 4, 5])),
]


def device_at(offset, core):
    cluster = lax.axis_index("cluster")
    blk = lax.axis_index("blk")
    x, y, z = blk % 4, cluster // 2, (cluster % 2) * 2 + blk // 4
    odd = z % 2
    dx, dy, dz = offset
    if TWIST == 1:
        dx, dy = dx - odd * (dx + dy), dy - odd * (dx + dy)
    elif TWIST == 2:
        dx, dy = dx + odd * (dy - dx), dy + odd * (dx - dy)
    elif TWIST == 3:
        dx, dy = dx - odd * (2 * dx), dy - odd * (2 * dy)
    elif TWIST == 4:
        dx = dx - odd * (2 * dx)
    x, y, z = (x + dx + 8) % 4, (y + dy + 8) % 4, (z + dz + 8) % 4
    return (y * 2 + z // 2, core, (z % 2) * 4 + x)


def send_groups():
    slots = len(SLOTS)
    columns = {(slot, piece) for slot, piece, _ in STEPS}
    pieces = len(SENDS) + len(columns)
    single_rows = len({dst for _, dst, _, _ in SENDS}) + len({slot for slot, _ in columns}) + 2 * slots - 1
    groups = []
    for count, each in ((pieces, 2 * PIECES), (single_rows, 2)):
        sizes = []
        while count >= each:
            sizes.append(min(count // each, slots) * each)
            count -= sizes[-1]
        groups.append(sizes + [1] * count)
    return groups


def kernel(
    x_ref, id_ref, o_ref, x_in, id_in, rows, ids, id_rows, row_best, col_best, partial, returned,
    load_sem, sent, sent_small, recv_sem, id_recv, twin_recv, twin_id_recv, home_recv,
):
    core = lax.axis_index("col")
    twin = 1 - core
    here = (0, 0, 0)
    slots = len(SLOTS)

    barrier = pltpu.get_barrier_semaphore()
    for direction in DIRECTIONS:
        pl.semaphore_signal(barrier, inc=1, device_id=device_at(direction, core), device_id_type=MESH)
    pl.semaphore_signal(barrier, inc=1, device_id=device_at(here, twin), device_id_type=MESH)
    load = pltpu.make_async_copy(x_ref, x_in, load_sem.at[0])
    load_ids = pltpu.make_async_copy(id_ref, id_in, load_sem.at[1])
    load.start()
    load_ids.start()

    def remote(src, dst, send, recv, device):
        return pltpu.make_async_remote_copy(
            src_ref=src, dst_ref=dst, send_sem=send, recv_sem=recv, device_id=device, device_id_type=MESH
        )

    def spread_ids(slot):
        for piece in range(PIECES):
            lane_ids = ids[slot, core, :, piece * PIECE:(piece + 1) * PIECE]
            id_rows[slot, piece] = jnp.broadcast_to(lane_ids, (PIECE, PIECE)).T

    piece_groups, row_groups = send_groups()
    piece_sems = iter([sent.at[g] for g, size in enumerate(piece_groups) for _ in range(size)])
    row_sems = iter([sent_small.at[g] for g, size in enumerate(row_groups) for _ in range(size)])

    def to_twin(slot, piece):
        copy = remote(
            rows.at[slot, piece, core], rows.at[slot, piece, core],
            next(piece_sems), twin_recv.at[slot, piece], device_at(here, twin),
        )
        copy.start()

    def ids_to_twin(slot):
        copy = remote(
            ids.at[slot, core], ids.at[slot, core], next(row_sems), twin_id_recv.at[slot],
            device_at(here, twin),
        )
        copy.start()

    def twin_wait(slot, piece):
        remote(
            rows.at[slot, piece, twin], rows.at[slot, piece, twin],
            sent.at[0], twin_recv.at[slot, piece], device_at(here, twin),
        ).wait_recv()

    def twin_ids_wait(slot):
        remote(
            ids.at[slot, twin], ids.at[slot, twin], sent_small.at[0], twin_id_recv.at[slot],
            device_at(here, twin),
        ).wait_recv()

    load_ids.wait()
    ids[0, core] = id_in[...].astype(jnp.float32)
    load.wait()
    features = x_in.shape[1]
    for piece in range(PIECES):
        values = x_in[piece * PIECE:(piece + 1) * PIECE].astype(jnp.float32)
        mean = jnp.mean(values * values, axis=-1, keepdims=True)
        scale = lax.rsqrt(mean + 1e-06) * (1.0 / features**0.5)
        rows[0, piece, core] = (values * scale).astype(jnp.bfloat16)
    pl.semaphore_wait(barrier, len(DIRECTIONS) + 1)

    twin_id_fresh = set()
    row_touched, col_touched, spread = set(), set(), set()

    def piece_copy(index, semaphore):
        src, dst, piece, direction = SENDS[index]
        return remote(
            rows.at[src, piece, core], rows.at[dst, piece, core],
            semaphore, recv_sem.at[dst, piece], device_at(DIRECTIONS[direction], core),
        )

    def id_copy(index, semaphore):
        src, dst, piece, direction = SENDS[index]
        return remote(
            ids.at[src, core], ids.at[dst, core], semaphore, id_recv.at[dst],
            device_at(DIRECTIONS[direction], core),
        )

    as_columns = {(slot, piece) for slot, piece, _ in STEPS}
    first_for = {}
    for kind, what in ORDER:
        if kind == 0:
            first_for.setdefault(SENDS[what][1], what)

    def arrive(index):
        src, dst, piece, direction = SENDS[index]
        if first_for[dst] == index:
            id_copy(index, sent_small.at[0]).wait_recv()
            if dst in {slot for slot, _ in as_columns}:
                ids_to_twin(dst)
        piece_copy(index, sent.at[0]).wait_recv()
        if (dst, piece) in as_columns:
            to_twin(dst, piece)

    def send(index):
        src, dst, piece, direction = SENDS[index]
        piece_copy(index, next(piece_sems)).start()
        if first_for[dst] == index:
            id_copy(index, next(row_sems)).start()

    def step(work):
        batch, before, after = work
        for index in batch:
            slot, piece, _ = STEPS[index]
            if slot not in twin_id_fresh:
                twin_id_fresh.add(slot)
                twin_ids_wait(slot)
            twin_wait(slot, piece)

        @pl.when(core < 2)
        def _():
            for slot in before:
                sum_up(slot)
            for index in batch:
                compare(*STEPS[index])
            for slot in after:
                sum_up(slot)

        for slot in before + after:
            for to_core in range(2 if slot else 1):
                home_copy(slot, to_core).start()

    def compare(slot, piece, others):
        own = [(0, p) for p in range(PIECES)] if slot == 0 else []
        pieces = others + own
        for s in sorted({s for s, _ in pieces} - spread):
            spread.add(s)
            spread_ids(s)
        columns = rows[slot, piece].reshape(2 * PIECE, features)
        stacked = jnp.concatenate([rows[s, p, core] for s, p in pieces], axis=0)
        scores = lax.dot_general(stacked, columns, NT, preferred_element_type=jnp.float32)
        lane_ids = [ids[slot, half, :, piece * PIECE:(piece + 1) * PIECE] for half in range(2)]
        columns_best = [None, None]
        for at, (s, p) in enumerate(pieces):
            row = row_best[s, p] if (s, p) in row_touched else None
            row_touched.add((s, p))
            for half in range(2):
                block = scores[at * PIECE:(at + 1) * PIECE, half * PIECE:(half + 1) * PIECE]
                allowed = id_rows[s, p] == lane_ids[half]
                if s == slot and p == piece:
                    r = lax.broadcasted_iota(jnp.int32, (PIECE, PIECE), 0)
                    c = lax.broadcasted_iota(jnp.int32, (PIECE, PIECE), 1)
                    allowed = allowed & (r + PIECE * core != c + PIECE * half)
                block = jnp.where(allowed, block, NEG)
                row = block if row is None else jnp.maximum(row, block)
                if s != slot:
                    best = jnp.max(block.reshape(PIECE // 8, 8, PIECE), axis=0)
                    seen = columns_best[half]
                    columns_best[half] = best if seen is None else jnp.maximum(seen, best)
            row_best[s, p] = row
        if columns_best[0] is not None:
            for half in range(2):
                col_best[slot, piece, half] = columns_best[half]
            col_touched.add((slot, piece))

    def home_copy(slot, to_core):
        if slot == 0:
            target, semaphore, device = returned.at[0, core], home_recv.at[0], device_at(here, twin)
            return remote(partial.at[0, twin], target, next(row_sems), semaphore, device)
        target, semaphore, device = returned.at[slot, core], home_recv.at[1], device_at(SLOTS[slot], to_core)
        return remote(partial.at[slot, to_core], target, next(row_sems), semaphore, device)

    def sum_up(slot):
        for piece in range(PIECES):
            mine = None
            if (slot, piece) in row_touched:
                mine = jnp.max(row_best[slot, piece].T, axis=0, keepdims=True)
            for half in range(2):
                best = jnp.full((1, PIECE), NEG, jnp.float32)
                if mine is not None:
                    best = jnp.where(core == half, mine, best)
                if (slot, piece) in col_touched:
                    best = jnp.maximum(best, jnp.max(col_best[slot, piece, half], axis=0, keepdims=True))
                partial[slot, half, :, piece * PIECE:(piece + 1) * PIECE] = best

    for piece in range(PIECES):
        to_twin(0, piece)
    ids_to_twin(0)
    for kind, what in ORDER:
        (arrive, send, step)[kind](what)

    def arrived(array, semaphore):
        remote(array, array, sent.at[0], semaphore, device_at(here, twin)).wait_recv()

    def left(array, semaphore):
        remote(array, array, semaphore, home_recv.at[0], device_at(here, twin)).wait_send()

    returned[0, core] = partial[0, core]
    arrived(returned.at[0, twin], home_recv.at[0])
    arrived(returned.at[1:slots], home_recv.at[1])
    o_ref[...] = jnp.max(returned[...], axis=(0, 1))
    for group, size in enumerate(piece_groups):
        whole = size // (2 * PIECES)
        left(rows.at[0:whole] if whole else rows.at[0, 0, 0], sent.at[group])
    for group, size in enumerate(row_groups):
        whole = size // 2
        left(ids.at[0:whole] if whole else ids.at[0, 0], sent_small.at[group])


def local(embeddings, assignment):
    count, features = embeddings.shape
    slots = len(SLOTS)
    dma = pltpu.SemaphoreType.DMA
    piece_groups, row_groups = send_groups()
    best = pl.pallas_call(
        kernel,
        out_shape=jax.ShapeDtypeStruct((1, count), jnp.float32),
        in_specs=[pl.BlockSpec(memory_space=pl.ANY)] * 2,
        out_specs=pl.BlockSpec(memory_space=pltpu.VMEM),
        scratch_shapes=[
            pltpu.VMEM((count, features), jnp.bfloat16),
            pltpu.VMEM((1, count), jnp.int32),
            pltpu.VMEM((slots, PIECES, 2, PIECE, features), jnp.bfloat16),
            pltpu.VMEM((slots, 2, 1, count), jnp.float32),
            pltpu.VMEM((slots, PIECES, PIECE, PIECE), jnp.float32),
            pltpu.VMEM((slots, PIECES, PIECE, PIECE), jnp.float32),
            pltpu.VMEM((slots, PIECES, 2, 8, PIECE), jnp.float32),
            pltpu.VMEM((slots, 2, 1, count), jnp.float32),
            pltpu.VMEM((slots, 2, 1, count), jnp.float32),
            dma((2,)),
            dma((len(piece_groups),)),
            dma((len(row_groups),)),
            dma((slots, PIECES)),
            dma((slots,)),
            dma((slots, PIECES)),
            dma((slots,)),
            dma((2,)),
        ],
        compiler_params=pltpu.CompilerParams(
            collective_id=0, has_side_effects=True, vmem_limit_bytes=56 * 2**20
        ),
    )(embeddings, assignment.reshape(1, count))
    return best.reshape(count)


def solution(mesh):
    axes = ("cluster", "col", "blk")
    return jax.shard_map(
        local, mesh=mesh, in_specs=(P(axes, None), P(axes, None)), out_specs=P(axes), check_vma=False
    )
```

```python
import jax
import jax.numpy as jnp
from jax import lax
from jax.experimental import pallas as pl
from jax.experimental.pallas import tpu as pltpu
from jax.sharding import PartitionSpec as P

MESH = pl.DeviceIdType.MESH
NT = (((1,), (1,)), ((), ()))
NEG = float("-inf")
PIECES = 3
PIECE = 128
DIRECTIONS = [(1, 0, 0), (-1, 0, 0), (0, 1, 0), (0, -1, 0), (0, 0, 1), (0, 0, -1)]
TWIST = 0
SLOTS = [
    (0, 0, 0), (0, 0, 1), (0, 0, 2), (0, 0, 3), (0, 1, 0), (0, 2, 0), (1, 0, 0), (1, 0, 2), (1, 0, 3), (3, 0, 0),
    (3, 1, 0), (3, 2, 0), (3, 3, 0),
]
SENDS = [
    (0, 9, 2, 0), (0, 6, 0, 1), (0, 4, 2, 3), (0, 3, 2, 4), (0, 1, 4, 5), (0, 9, 3, 0), (0, 6, 1, 1), (0, 4, 3, 3),
    (0, 3, 3, 4), (0, 1, 5, 5), (0, 9, 4, 0), (0, 6, 2, 1), (0, 4, 0, 3), (0, 3, 4, 4), (0, 1, 0, 5), (0, 9, 5, 0),
    (0, 6, 3, 1), (0, 4, 1, 3), (0, 3, 5, 4), (0, 1, 1, 5), (0, 9, 0, 0), (0, 6, 4, 1), (0, 4, 4, 3), (0, 3, 0, 4),
    (0, 1, 2, 5), (9, 12, 2, 2), (4, 10, 2, 0), (0, 6, 5, 1), (4, 5, 2, 3), (0, 3, 1, 4), (0, 1, 3, 5), (9, 12, 3,
    2), (4, 10, 3, 0), (3, 8, 2, 1), (4, 5, 3, 3), (6, 8, 0, 4), (1, 2, 4, 5), (9, 12, 4, 2), (4, 10, 0, 0), (3, 8,
    3, 1), (4, 5, 0, 3), (6, 8, 1, 4), (1, 2, 5, 5), (9, 12, 5, 2), (4, 10, 1, 0), (3, 8, 4, 1), (4, 5, 1, 3), (1,
    2, 0, 5), (9, 12, 0, 2), (4, 10, 4, 0), (3, 8, 5, 1), (12, 11, 4, 2), (4, 5, 4, 3), (1, 2, 1, 5), (0, 9, 1, 0),
    (12, 11, 5, 2), (9, 10, 5, 3), (1, 2, 2, 5), (8, 7, 2, 4), (8, 7, 0, 4), (2, 7, 4, 1), (12, 11, 0, 2), (10, 11,
    2, 3), (1, 2, 3, 5), (8, 7, 3, 4), (2, 7, 5, 1), (10, 11, 3, 3), (8, 7, 1, 4), (5, 11, 1, 0), (11, 5, 5, 1), (0,
    4, 5, 3), (9, 12, 1, 2),
]
STEPS = [
    (0, 0, []),
    (0, 1, []),
    (0, 2, []),
    (9, 1, [(0, 0), (0, 1), (0, 2), (1, 2), (3, 1), (4, 1), (6, 0)]),
    (4, 1, [(0, 0), (0, 1), (0, 2), (1, 2), (3, 1), (6, 0)]),
    (3, 1, [(0, 0), (0, 1), (0, 2), (1, 2), (6, 0)]),
    (6, 0, [(0, 0), (0, 2), (1, 0), (1, 2), (3, 2), (4, 0), (9, 2)]),
    (1, 2, [(0, 0), (0, 2), (3, 2), (4, 0), (6, 1), (9, 2)]),
    (6, 1, [(0, 0), (0, 2), (1, 0), (3, 1), (3, 2), (4, 0), (4, 1), (9, 1), (9, 2), (12, 1)]),
    (4, 0, [(0, 0), (0, 1), (0, 2), (1, 0), (3, 1), (3, 2), (9, 1), (9, 2), (12, 1)]),
    (3, 2, [(0, 0), (0, 1), (1, 0), (4, 1), (9, 1), (9, 2), (12, 1)]),
    (1, 0, [(0, 0), (3, 0), (3, 1), (4, 1), (6, 2), (12, 1)]),
    (9, 2, [(0, 2), (4, 1), (6, 2), (12, 1)]),
    (12, 1, [(0, 2), (1, 1), (1, 2), (3, 0), (3, 1), (4, 1), (6, 0), (6, 2)]),
    (3, 0, [(0, 1), (4, 0), (4, 1), (5, 1), (6, 0), (6, 1), (6, 2), (9, 1), (10, 1), (12, 2)]),
    (6, 2, [(0, 0), (4, 0), (4, 1), (5, 1), (10, 1), (12, 2)]),
    (1, 1, [(3, 1), (4, 0), (4, 1), (5, 1), (10, 1), (12, 2)]),
    (12, 2, [(0, 2), (1, 0), (1, 2), (2, 2), (3, 1), (3, 2), (4, 0), (4, 1), (5, 1), (6, 0), (8, 0), (8, 1), (9, 2), (10, 1)]),
    (10, 1, [(1, 0), (1, 2), (2, 2), (3, 1), (3, 2), (6, 0), (8, 0), (8, 1), (12, 1)]),
    (5, 1, [(0, 0), (1, 0), (1, 2), (2, 2), (3, 2), (8, 0), (8, 1)]),
    (8, 1, [(1, 0), (1, 1), (1, 2), (4, 0), (5, 0), (9, 1), (9, 2), (10, 0), (12, 1)]),
    (8, 0, [(1, 0), (1, 1), (1, 2), (4, 0), (5, 0), (9, 1), (9, 2), (10, 0), (12, 1)]),
    (2, 2, [(4, 0), (4, 1), (5, 0), (6, 2), (9, 1), (10, 0), (12, 1)]),
    (5, 0, [(0, 0), (0, 2), (1, 0), (1, 2), (2, 0), (3, 2), (6, 0), (6, 1), (6, 2), (8, 2), (10, 0), (12, 2)]),
    (10, 0, [(1, 0), (1, 1), (1, 2), (2, 0), (3, 2), (5, 1), (6, 0), (8, 2), (11, 2)]),
    (11, 2, [(0, 2), (1, 0), (1, 1), (1, 2), (2, 0), (2, 2), (3, 0), (3, 1), (3, 2), (6, 0), (6, 1), (6, 2), (8, 0), (8, 1), (8, 2), (9, 2)]),
    (8, 2, [(1, 0), (5, 1), (9, 0), (9, 1), (9, 2), (10, 1), (10, 2), (12, 1), (12, 2)]),
    (2, 0, [(4, 0), (4, 1), (5, 1), (10, 1), (10, 2), (11, 0), (12, 1), (12, 2)]),
    (10, 2, [(0, 2), (1, 0), (1, 1), (1, 2), (2, 1), (2, 2), (3, 0), (3, 1), (3, 2), (6, 0), (7, 1), (7, 2), (8, 0), (8, 1)]),
    (9, 0, [(6, 0), (7, 1), (7, 2), (8, 0), (8, 1)]),
    (7, 1, [(4, 0), (4, 1), (5, 0), (5, 1), (5, 2), (9, 1), (9, 2), (10, 0), (10, 1), (11, 0), (11, 1), (11, 2), (12, 2)]),
    (11, 0, [(1, 0), (1, 1), (1, 2), (2, 2), (6, 0), (6, 1), (7, 0), (7, 2), (8, 0), (8, 1), (8, 2)]),
    (2, 1, [(4, 0), (4, 1), (5, 1), (12, 1), (12, 2)]),
    (7, 2, [(5, 1), (9, 2), (10, 0), (11, 2), (12, 0)]),
    (11, 1, [(1, 0), (1, 1), (1, 2), (2, 0), (6, 1), (8, 0), (8, 1), (8, 2)]),
    (7, 0, [(9, 0), (10, 0), (10, 1)]),
    (5, 2, [(1, 2), (2, 2), (10, 0)]),
    (12, 0, [(1, 0), (1, 1), (1, 2), (2, 0), (2, 1), (2, 2), (3, 0), (3, 1), (3, 2), (8, 0), (8, 1), (8, 2)]),
    (4, 2, [(1, 0), (1, 1), (1, 2), (2, 0), (2, 1), (2, 2), (3, 0), (3, 1), (3, 2)]),
]
ORDER = [
    (1, 0),
    (1, 1),
    (1, 2),
    (1, 3),
    (1, 4),
    (1, 5),
    (1, 6),
    (1, 7),
    (1, 8),
    (1, 9),
    (1, 10),
    (1, 11),
    (1, 12),
    (1, 13),
    (1, 14),
    (2, ([0, 1, 2], [], [])),
    (1, 15),
    (1, 16),
    (1, 17),
    (1, 18),
    (1, 19),
    (1, 20),
    (1, 21),
    (1, 22),
    (1, 23),
    (1, 24),
    (0, 0),
    (1, 25),
    (0, 1),
    (0, 2),
    (0, 3),
    (0, 4),
    (1, 26),
    (1, 27),
    (1, 28),
    (1, 29),
    (1, 30),
    (0, 5),
    (1, 31),
    (0, 6),
    (0, 7),
    (0, 8),
    (0, 9),
    (1, 32),
    (1, 33),
    (1, 34),
    (1, 35),
    (1, 36),
    (0, 10),
    (1, 37),
    (0, 11),
    (0, 12),
    (0, 13),
    (0, 14),
    (2, ([3, 4, 5], [], [])),
    (0, 25),
    (1, 38),
    (1, 39),
    (1, 40),
    (1, 41),
    (1, 42),
    (0, 15),
    (1, 43),
    (0, 16),
    (0, 17),
    (0, 18),
    (0, 19),
    (2, ([6, 7], [], [])),
    (1, 44),
    (1, 45),
    (0, 31),
    (1, 46),
    (1, 47),
    (0, 20),
    (1, 48),
    (0, 21),
    (0, 22),
    (0, 23),
    (0, 24),
    (2, ([8, 9, 10], [], [])),
    (0, 37),
    (1, 49),
    (1, 50),
    (1, 51),
    (1, 52),
    (1, 53),
    (0, 26),
    (0, 27),
    (0, 28),
    (0, 29),
    (0, 30),
    (2, ([11, 12, 13], [], [])),
    (0, 43),
    (1, 54),
    (1, 55),
    (1, 56),
    (1, 57),
    (0, 32),
    (0, 33),
    (1, 58),
    (0, 34),
    (0, 35),
    (1, 59),
    (0, 36),
    (1, 60),
    (2, ([14, 15, 16], [], [])),
    (0, 48),
    (1, 61),
    (1, 62),
    (1, 63),
    (0, 38),
    (0, 39),
    (1, 64),
    (0, 40),
    (0, 41),
    (0, 42),
    (1, 65),
    (2, ([17, 18, 19], [], [])),
    (0, 51),
    (1, 66),
    (1, 67),
    (0, 44),
    (0, 45),
    (0, 46),
    (1, 68),
    (0, 47),
    (2, ([20, 21, 22], [], [])),
    (0, 55),
    (1, 69),
    (1, 70),
    (0, 58),
    (0, 49),
    (0, 50),
    (0, 52),
    (0, 53),
    (2, ([23, 24], [], [])),
    (0, 61),
    (0, 59),
    (0, 54),
    (1, 71),
    (0, 60),
    (0, 56),
    (0, 57),
    (2, ([25, 26], [], [])),
    (0, 64),
    (0, 65),
    (0, 62),
    (0, 63),
    (0, 68),
    (2, ([27, 28, 29], [], [])),
    (0, 67),
    (0, 69),
    (0, 66),
    (2, ([30, 31, 32], [0], [])),
    (0, 71),
    (0, 70),
    (2, ([33, 34, 35], [], [])),
    (2, ([36], [11, 7, 6, 9], [])),
    (2, ([37], [5, 10], [])),
    (2, ([38], [12, 8], [2, 1, 3, 4])),
]


def device_at(offset, core):
    cluster = lax.axis_index("cluster")
    blk = lax.axis_index("blk")
    x, y, z = blk % 4, cluster // 2, (cluster % 2) * 2 + blk // 4
    odd = z % 2
    dx, dy, dz = offset
    if TWIST == 1:
        dx, dy = dx - odd * (dx + dy), dy - odd * (dx + dy)
    elif TWIST == 2:
        dx, dy = dx + odd * (dy - dx), dy + odd * (dx - dy)
    elif TWIST == 3:
        dx, dy = dx - odd * (2 * dx), dy - odd * (2 * dy)
    elif TWIST == 4:
        dx = dx - odd * (2 * dx)
    x, y, z = (x + dx + 8) % 4, (y + dy + 8) % 4, (z + dz + 8) % 4
    return (y * 2 + z // 2, core, (z % 2) * 4 + x)


def send_groups():
    halves = len(SENDS)
    slots = len(SLOTS)
    columns = {(slot, piece) for slot, piece, _ in STEPS}
    pieces = len(columns)
    single_rows = len({dst for _, dst, _, _ in SENDS}) + len({slot for slot, _ in columns}) + 2 * slots - 1
    groups = []
    for count, each in ((pieces, 2 * PIECES), (single_rows, 2), (halves, 4 * PIECES)):
        sizes = []
        while count >= each:
            sizes.append(min(count // each, slots) * each)
            count -= sizes[-1]
        groups.append(sizes + [1] * count)
    return groups


def kernel(
    x_ref, id_ref, o_ref, x_in, id_in, rows, ids, id_rows, row_best, col_best, partial, returned,
    load_sem, sent, sent_small, sent_half, recv_sem, id_recv, twin_recv, twin_id_recv, home_recv,
):
    core = lax.axis_index("col")
    twin = 1 - core
    here = (0, 0, 0)
    neighbours = [device_at(direction, core) for direction in DIRECTIONS]
    other_core = device_at(here, twin)
    slots = len(SLOTS)

    barrier = pltpu.get_barrier_semaphore()
    for device in neighbours + [other_core]:
        pl.semaphore_signal(barrier, inc=1, device_id=device, device_id_type=MESH)
    load = pltpu.make_async_copy(x_ref, x_in, load_sem.at[0])
    load_ids = pltpu.make_async_copy(id_ref, id_in, load_sem.at[1])
    load.start()
    load_ids.start()

    def remote(src, dst, send, recv, device):
        return pltpu.make_async_remote_copy(
            src_ref=src, dst_ref=dst, send_sem=send, recv_sem=recv, device_id=device, device_id_type=MESH
        )

    def spread_ids(slot):
        for piece in range(PIECES):
            lane_ids = ids[slot, core, :, piece * PIECE:(piece + 1) * PIECE]
            id_rows[slot, piece] = jnp.broadcast_to(lane_ids, (PIECE, PIECE)).T

    piece_groups, row_groups, half_groups = send_groups()
    piece_sems = iter([sent.at[g] for g, size in enumerate(piece_groups) for _ in range(size)])
    half_sems = iter([sent_half.at[g] for g, size in enumerate(half_groups) for _ in range(size)])
    row_sems = iter([sent_small.at[g] for g, size in enumerate(row_groups) for _ in range(size)])

    def to_twin(slot, piece):
        copy = remote(
            rows.at[slot, piece, core], rows.at[slot, piece, core],
            next(piece_sems), twin_recv.at[slot, piece], other_core,
        )
        copy.start()

    def ids_to_twin(slot):
        copy = remote(
            ids.at[slot, core], ids.at[slot, core], next(row_sems), twin_id_recv.at[slot],
            other_core,
        )
        copy.start()

    def twin_wait(slot, piece):
        remote(
            rows.at[slot, piece, twin], rows.at[slot, piece, twin],
            sent.at[0], twin_recv.at[slot, piece], other_core,
        ).wait_recv()

    def twin_ids_wait(slot):
        remote(
            ids.at[slot, twin], ids.at[slot, twin], sent_small.at[0], twin_id_recv.at[slot],
            other_core,
        ).wait_recv()

    load_ids.wait()
    ids[0, core] = id_in[...].astype(jnp.float32)
    load.wait()
    features = x_in.shape[1]
    for piece in range(PIECES):
        values = x_in[piece * PIECE:(piece + 1) * PIECE].astype(jnp.float32)
        mean = jnp.mean(values * values, axis=-1, keepdims=True)
        scale = lax.rsqrt(mean + 1e-06) * (1.0 / features**0.5)
        rows[0, piece, core] = (values * scale).astype(jnp.bfloat16)
    pl.semaphore_wait(barrier, len(DIRECTIONS) + 1)

    twin_id_fresh = set()
    row_touched, col_touched, spread = set(), set(), set()

    def half_copy(index, semaphore):
        src, dst, half, direction = SENDS[index]
        place = pl.ds(half % 2 * (PIECE // 2), PIECE // 2)
        return remote(
            rows.at[src, half // 2, core, place], rows.at[dst, half // 2, core, place],
            semaphore, recv_sem.at[dst, half], neighbours[direction],
        )

    def id_copy(index, semaphore):
        src, dst, half, direction = SENDS[index]
        return remote(
            ids.at[src, core], ids.at[dst, core], semaphore, id_recv.at[dst],
            neighbours[direction],
        )

    as_columns = {(slot, piece) for slot, piece, _ in STEPS}
    have = set()
    for_twin = [(0, piece) for piece in range(PIECES)] + [(0, None)]

    def serve_twin():
        while for_twin:
            slot, piece = for_twin.pop(0)
            if piece is None:
                ids_to_twin(slot)
            else:
                to_twin(slot, piece)

    first_for = {}
    for kind, what in ORDER:
        if kind == 0:
            first_for.setdefault(SENDS[what][1], what)

    def arrive(index):
        src, dst, half, direction = SENDS[index]
        if first_for[dst] == index:
            id_copy(index, sent_small.at[0]).wait_recv()
            if dst in {slot for slot, _ in as_columns}:
                for_twin.append((dst, None))
        half_copy(index, sent.at[0]).wait_recv()
        have.add((dst, half))
        if (dst, half ^ 1) in have and (dst, half // 2) in as_columns:
            for_twin.append((dst, half // 2))

    def send(index):
        src, dst, half, direction = SENDS[index]
        half_copy(index, next(half_sems)).start()
        if first_for[dst] == index:
            id_copy(index, next(row_sems)).start()

    def step(work):
        batch, before, after = work
        for index in batch:
            slot, piece, _ = STEPS[index]
            if slot not in twin_id_fresh:
                twin_id_fresh.add(slot)
                twin_ids_wait(slot)
            twin_wait(slot, piece)

        @pl.when(core < 2)
        def _():
            for slot in before:
                sum_up(slot)
            for index in batch:
                compare(*STEPS[index])
            for slot in after:
                sum_up(slot)

        for slot in before + after:
            for to_core in range(2 if slot else 1):
                home_copy(slot, to_core).start()

    def compare(slot, piece, others):
        own = [(0, p) for p in range(PIECES)] if slot == 0 else []
        pieces = others + own
        for s in sorted({s for s, _ in pieces} - spread):
            spread.add(s)
            spread_ids(s)
        columns = rows[slot, piece].reshape(2 * PIECE, features)
        stacked = jnp.concatenate([rows[s, p, core] for s, p in pieces], axis=0)
        scores = lax.dot_general(stacked, columns, NT, preferred_element_type=jnp.float32)
        lane_ids = [ids[slot, half, :, piece * PIECE:(piece + 1) * PIECE] for half in range(2)]
        columns_best = [None, None]
        for at, (s, p) in enumerate(pieces):
            row = row_best[s, p] if (s, p) in row_touched else None
            row_touched.add((s, p))
            for half in range(2):
                block = scores[at * PIECE:(at + 1) * PIECE, half * PIECE:(half + 1) * PIECE]
                allowed = id_rows[s, p] == lane_ids[half]
                if s == slot and p == piece:
                    r = lax.broadcasted_iota(jnp.int32, (PIECE, PIECE), 0)
                    c = lax.broadcasted_iota(jnp.int32, (PIECE, PIECE), 1)
                    allowed = allowed & (r + PIECE * core != c + PIECE * half)
                block = jnp.where(allowed, block, NEG)
                row = block if row is None else jnp.maximum(row, block)
                if s != slot:
                    best = jnp.max(block.reshape(PIECE // 8, 8, PIECE), axis=0)
                    seen = columns_best[half]
                    columns_best[half] = best if seen is None else jnp.maximum(seen, best)
            row_best[s, p] = row
        if columns_best[0] is not None:
            for half in range(2):
                col_best[slot, piece, half] = columns_best[half]
            col_touched.add((slot, piece))

    def home_copy(slot, to_core):
        if slot == 0:
            target, semaphore, device = returned.at[0, core], home_recv.at[0], other_core
            return remote(partial.at[0, twin], target, next(row_sems), semaphore, device)
        target, semaphore, device = returned.at[slot, core], home_recv.at[1], device_at(SLOTS[slot], to_core)
        return remote(partial.at[slot, to_core], target, next(row_sems), semaphore, device)

    def sum_up(slot):
        for piece in range(PIECES):
            mine = None
            if (slot, piece) in row_touched:
                mine = jnp.max(row_best[slot, piece].T, axis=0, keepdims=True)
            for half in range(2):
                best = jnp.full((1, PIECE), NEG, jnp.float32)
                if mine is not None:
                    best = jnp.where(core == half, mine, best)
                if (slot, piece) in col_touched:
                    best = jnp.maximum(best, jnp.max(col_best[slot, piece, half], axis=0, keepdims=True))
                partial[slot, half, :, piece * PIECE:(piece + 1) * PIECE] = best

    for kind, what in ORDER:
        if kind != 1:
            serve_twin()
        (arrive, send, step)[kind](what)

    def arrived(array, semaphore):
        remote(array, array, sent.at[0], semaphore, other_core).wait_recv()

    def left(array, semaphore):
        remote(array, array, semaphore, home_recv.at[0], other_core).wait_send()

    returned[0, core] = partial[0, core]
    arrived(returned.at[0, twin], home_recv.at[0])
    arrived(returned.at[1:slots], home_recv.at[1])
    o_ref[...] = jnp.max(returned[...], axis=(0, 1))
    for group, size in enumerate(piece_groups):
        whole = size // (2 * PIECES)
        left(rows.at[0:whole] if whole else rows.at[0, 0, 0], sent.at[group])
    for group, size in enumerate(half_groups):
        whole = size // (4 * PIECES)
        left(rows.at[0:whole] if whole else rows.at[0, 0, 0, 0:PIECE // 2], sent_half.at[group])
    for group, size in enumerate(row_groups):
        whole = size // 2
        left(ids.at[0:whole] if whole else ids.at[0, 0], sent_small.at[group])


def local(embeddings, assignment):
    count, features = embeddings.shape
    slots = len(SLOTS)
    dma = pltpu.SemaphoreType.DMA
    piece_groups, row_groups, half_groups = send_groups()
    best = pl.pallas_call(
        kernel,
        out_shape=jax.ShapeDtypeStruct((1, count), jnp.float32),
        in_specs=[pl.BlockSpec(memory_space=pl.ANY)] * 2,
        out_specs=pl.BlockSpec(memory_space=pltpu.VMEM),
        scratch_shapes=[
            pltpu.VMEM((count, features), jnp.bfloat16),
            pltpu.VMEM((1, count), jnp.int32),
            pltpu.VMEM((slots, PIECES, 2, PIECE, features), jnp.bfloat16),
            pltpu.VMEM((slots, 2, 1, count), jnp.float32),
            pltpu.VMEM((slots, PIECES, PIECE, PIECE), jnp.float32),
            pltpu.VMEM((slots, PIECES, PIECE, PIECE), jnp.float32),
            pltpu.VMEM((slots, PIECES, 2, 8, PIECE), jnp.float32),
            pltpu.VMEM((slots, 2, 1, count), jnp.float32),
            pltpu.VMEM((slots, 2, 1, count), jnp.float32),
            dma((2,)),
            dma((len(piece_groups),)),
            dma((len(row_groups),)),
            dma((len(half_groups),)),
            dma((slots, 2 * PIECES)),
            dma((slots,)),
            dma((slots, PIECES)),
            dma((slots,)),
            dma((2,)),
        ],
        compiler_params=pltpu.CompilerParams(
            collective_id=0, has_side_effects=True, vmem_limit_bytes=56 * 2**20
        ),
    )(embeddings, assignment.reshape(1, count))
    return best.reshape(count)


def solution(mesh):
    axes = ("cluster", "col", "blk")
    return jax.shard_map(
        local, mesh=mesh, in_specs=(P(axes, None), P(axes, None)), out_specs=P(axes), check_vma=False
    )
```

```python
import jax
import jax.numpy as jnp
from jax import lax
from jax.experimental import pallas as pl
from jax.experimental.pallas import tpu as pltpu
from jax.sharding import PartitionSpec as P

MESH = pl.DeviceIdType.MESH
NT = (((1,), (1,)), ((), ()))
NEG = float("-inf")
PIECES = 3
PIECE = 128
DIRECTIONS = [(1, 0, 0), (-1, 0, 0), (0, 1, 0), (0, -1, 0), (0, 0, 1), (0, 0, -1)]
TWIST = 0
SLOTS = [
    (0, 0, 0), (0, 0, 1), (0, 0, 2), (0, 0, 3), (0, 1, 0), (0, 2, 0), (1, 0, 0), (1, 0, 2), (1, 0, 3), (1, 1, 3),
    (3, 0, 0), (3, 1, 0), (3, 2, 0), (3, 3, 0),
]
SENDS = [
    (0, 10, 4, 0), (0, 6, 2, 1), (0, 4, 2, 3), (0, 3, 4, 4), (0, 1, 0, 5), (0, 10, 5, 0), (0, 6, 3, 1), (0, 4, 3,
    3), (0, 3, 5, 4), (0, 1, 1, 5), (0, 10, 2, 0), (0, 6, 4, 1), (0, 4, 0, 3), (0, 3, 0, 4), (0, 1, 2, 5), (0, 10,
    3, 0), (0, 6, 5, 1), (0, 4, 1, 3), (0, 3, 1, 4), (0, 1, 3, 5), (0, 10, 0, 0), (0, 6, 0, 1), (0, 4, 4, 3), (0, 1,
    4, 5), (10, 13, 4, 2), (6, 8, 2, 4), (0, 10, 1, 0), (0, 6, 1, 1), (4, 5, 2, 3), (0, 1, 5, 5), (10, 13, 5, 2),
    (6, 8, 3, 4), (3, 8, 4, 1), (4, 5, 3, 3), (1, 2, 0, 5), (10, 13, 2, 2), (4, 11, 0, 0), (3, 8, 0, 1), (13, 12, 4,
    2), (4, 5, 0, 3), (1, 2, 2, 5), (10, 13, 3, 2), (6, 8, 5, 4), (4, 11, 1, 0), (3, 2, 1, 4), (3, 8, 1, 1), (13,
    12, 5, 2), (4, 5, 1, 3), (1, 2, 3, 5), (4, 11, 4, 0), (8, 7, 2, 4), (10, 13, 0, 2), (8, 9, 2, 3), (1, 2, 4, 5),
    (5, 12, 2, 0), (8, 7, 3, 4), (12, 5, 4, 1), (10, 13, 1, 2), (8, 9, 3, 3), (1, 2, 5, 5), (8, 7, 4, 4), (5, 12, 3,
    0), (2, 7, 0, 1), (11, 12, 0, 3), (8, 7, 5, 4), (2, 7, 1, 1), (2, 3, 2, 5), (12, 5, 5, 1), (12, 11, 5, 2), (11,
    12, 1, 3), (2, 3, 3, 5), (0, 4, 5, 3), (12, 11, 2, 2), (12, 11, 3, 2),
]
STEPS = [
    (0, 0, []),
    (0, 1, []),
    (0, 2, []),
    (10, 2, [(0, 0), (0, 1), (0, 2), (1, 0), (3, 2), (4, 1), (6, 1)]),
    (4, 1, [(0, 0), (0, 1), (0, 2), (1, 0), (3, 2), (6, 1)]),
    (6, 1, [(0, 0), (0, 1), (1, 0), (3, 2)]),
    (3, 2, [(0, 0), (0, 1), (0, 2), (1, 0), (1, 1), (4, 0), (6, 2), (10, 1)]),
    (1, 0, [(0, 0), (0, 1), (3, 0), (4, 0), (6, 2), (10, 1)]),
    (4, 0, [(0, 0), (0, 1), (0, 2), (1, 1), (3, 0), (6, 1), (6, 2), (10, 1), (10, 2), (13, 2)]),
    (3, 0, [(0, 1), (0, 2), (1, 1), (4, 1), (6, 1), (6, 2), (10, 1), (10, 2), (13, 2)]),
    (10, 1, [(0, 0), (0, 2), (1, 1), (4, 1), (6, 1)]),
    (6, 2, [(0, 0), (4, 1), (8, 1), (10, 0), (10, 2), (13, 2)]),
    (1, 1, [(0, 1), (4, 1), (6, 1), (8, 1), (13, 2)]),
    (13, 2, [(0, 2), (1, 0), (1, 2), (3, 2), (4, 1), (6, 0), (6, 1), (8, 1), (10, 2)]),
    (10, 0, [(0, 0), (1, 0), (3, 0), (4, 0), (4, 1), (5, 1), (6, 0), (6, 1), (8, 1), (8, 2)]),
    (8, 1, [(0, 2), (1, 0), (1, 2), (4, 0), (4, 1), (5, 1), (10, 1), (10, 2)]),
    (1, 2, [(3, 2), (4, 0), (4, 1), (5, 1), (8, 2), (10, 1)]),
    (6, 0, [(2, 0), (4, 0), (4, 1), (5, 1), (11, 0), (13, 1)]),
    (5, 1, [(0, 0), (0, 1), (0, 2), (1, 0), (1, 1), (2, 0), (3, 0), (3, 2), (6, 1), (6, 2), (8, 2), (13, 2)]),
    (8, 2, [(1, 0), (1, 1), (4, 0), (4, 1), (10, 1), (10, 2), (11, 0), (13, 1), (13, 2)]),
    (13, 1, [(0, 2), (1, 0), (1, 1), (1, 2), (2, 0), (2, 1), (3, 0), (3, 2), (6, 1), (6, 2), (8, 0), (8, 1), (10, 2)]),
    (11, 0, [(1, 0), (1, 1), (1, 2), (2, 0), (2, 1), (3, 0), (8, 0), (8, 1), (12, 2), (13, 2)]),
    (2, 0, [(4, 0), (4, 1), (5, 0), (10, 1), (10, 2), (12, 2), (13, 2)]),
    (12, 2, [(0, 2), (1, 0), (1, 1), (1, 2), (2, 1), (3, 0), (3, 2), (4, 0), (6, 0), (6, 1), (6, 2), (7, 1), (8, 0), (8, 1), (8, 2), (10, 2)]),
    (5, 0, [(0, 0), (1, 0), (1, 2), (3, 2), (6, 0), (6, 2), (7, 1), (8, 0), (8, 1), (8, 2)]),
    (8, 0, [(4, 1), (5, 1), (10, 0), (10, 1), (10, 2), (13, 2)]),
    (2, 1, [(0, 1), (4, 0), (4, 1), (5, 1), (12, 1), (13, 0), (13, 2)]),
    (7, 1, [(4, 1), (9, 1), (10, 0), (10, 1), (10, 2), (11, 0), (12, 1), (13, 0), (13, 1), (13, 2)]),
    (13, 0, [(0, 2), (1, 0), (1, 1), (1, 2), (2, 0), (2, 2), (3, 0), (3, 2), (6, 1), (6, 2), (7, 0), (7, 2), (8, 0), (8, 1), (8, 2), (9, 1)]),
    (12, 1, [(1, 0), (1, 1), (1, 2), (2, 0), (2, 2), (6, 0), (6, 1), (7, 0), (8, 0), (8, 1), (8, 2), (9, 1)]),
    (2, 2, [(4, 0), (4, 1), (5, 0), (5, 1), (5, 2), (11, 0), (11, 2), (12, 0), (12, 2), (13, 1), (13, 2)]),
    (11, 2, [(0, 2), (1, 0), (1, 1), (1, 2), (2, 0), (2, 1), (3, 0), (3, 1), (3, 2), (7, 1), (7, 2), (8, 0), (8, 1), (8, 2)]),
    (9, 1, [(0, 0), (0, 1), (0, 2)]),
    (7, 0, [(4, 1), (5, 0), (10, 0), (10, 2), (12, 0), (12, 2), (13, 2)]),
    (7, 2, [(4, 1), (10, 2), (12, 2)]),
    (12, 0, [(1, 0), (1, 1), (1, 2), (6, 0), (8, 0), (8, 2)]),
    (5, 2, [(1, 2), (8, 1)]),
    (3, 1, [(4, 0), (4, 2)]),
    (4, 2, [(1, 0), (1, 1), (1, 2), (2, 0), (2, 1), (2, 2), (3, 0), (3, 2)]),
    (11, 1, [(1, 0), (1, 1), (1, 2), (8, 0), (8, 2)]),
]
ORDER = [
    (1, 0),
    (1, 1),
    (1, 2),
    (1, 3),
    (1, 4),
    (1, 5),
    (1, 6),
    (1, 7),
    (1, 8),
    (1, 9),
    (1, 10),
    (1, 11),
    (1, 12),
    (1, 13),
    (1, 14),
    (2, ([0, 1, 2], [], [])),
    (1, 15),
    (1, 16),
    (1, 17),
    (1, 18),
    (1, 19),
    (1, 20),
    (1, 21),
    (1, 22),
    (1, 23),
    (0, 0),
    (1, 24),
    (0, 1),
    (1, 25),
    (0, 2),
    (0, 3),
    (0, 4),
    (1, 26),
    (1, 27),
    (1, 28),
    (1, 29),
    (0, 5),
    (1, 30),
    (0, 6),
    (1, 31),
    (0, 7),
    (0, 8),
    (0, 9),
    (1, 32),
    (1, 33),
    (1, 34),
    (0, 10),
    (1, 35),
    (0, 11),
    (0, 12),
    (1, 36),
    (0, 13),
    (0, 14),
    (2, ([3, 4, 5], [], [])),
    (0, 24),
    (1, 37),
    (1, 38),
    (1, 39),
    (1, 40),
    (0, 15),
    (1, 41),
    (0, 16),
    (1, 42),
    (0, 17),
    (1, 43),
    (0, 18),
    (1, 44),
    (0, 19),
    (2, ([6, 7], [], [])),
    (0, 30),
    (1, 45),
    (1, 46),
    (1, 47),
    (1, 48),
    (0, 20),
    (0, 21),
    (0, 22),
    (1, 49),
    (0, 25),
    (1, 50),
    (0, 23),
    (2, ([8, 9, 10], [], [])),
    (0, 35),
    (1, 51),
    (1, 52),
    (1, 53),
    (0, 26),
    (0, 27),
    (0, 28),
    (1, 54),
    (0, 31),
    (1, 55),
    (0, 29),
    (2, ([11, 12, 13], [], [])),
    (0, 38),
    (1, 56),
    (1, 57),
    (1, 58),
    (1, 59),
    (0, 36),
    (0, 32),
    (1, 60),
    (0, 33),
    (1, 61),
    (0, 42),
    (0, 34),
    (1, 62),
    (2, ([14, 15, 16], [], [])),
    (0, 41),
    (1, 63),
    (1, 64),
    (0, 43),
    (0, 37),
    (0, 39),
    (0, 44),
    (1, 65),
    (0, 40),
    (1, 66),
    (2, ([17, 18, 19], [], [])),
    (0, 46),
    (1, 67),
    (1, 68),
    (1, 69),
    (0, 49),
    (0, 45),
    (0, 47),
    (0, 50),
    (0, 48),
    (1, 70),
    (2, ([20, 21, 22], [], [])),
    (0, 51),
    (1, 71),
    (0, 54),
    (1, 72),
    (0, 56),
    (0, 52),
    (0, 55),
    (0, 53),
    (2, ([23, 24, 25], [], [])),
    (0, 57),
    (0, 61),
    (1, 73),
    (0, 62),
    (0, 58),
    (0, 60),
    (0, 59),
    (2, ([26, 27], [], [])),
    (0, 68),
    (0, 65),
    (0, 63),
    (0, 64),
    (0, 66),
    (2, ([28, 29], [], [])),
    (0, 67),
    (0, 69),
    (0, 70),
    (0, 72),
    (2, ([30, 31, 32], [], [])),
    (0, 71),
    (0, 73),
    (2, ([33, 34, 35], [9, 0], [])),
    (2, ([36, 37], [7, 12, 13, 10, 6], [])),
    (2, ([38, 39], [5], [2, 8, 11, 3, 4, 1])),
]


def device_at(offset, core):
    cluster = lax.axis_index("cluster")
    blk = lax.axis_index("blk")
    x, y, z = blk % 4, cluster // 2, (cluster % 2) * 2 + blk // 4
    odd = z % 2
    dx, dy, dz = offset
    if TWIST == 1:
        dx, dy = dx - odd * (dx + dy), dy - odd * (dx + dy)
    elif TWIST == 2:
        dx, dy = dx + odd * (dy - dx), dy + odd * (dx - dy)
    elif TWIST == 3:
        dx, dy = dx - odd * (2 * dx), dy - odd * (2 * dy)
    elif TWIST == 4:
        dx = dx - odd * (2 * dx)
    x, y, z = (x + dx + 8) % 4, (y + dy + 8) % 4, (z + dz + 8) % 4
    return (y * 2 + z // 2, core, (z % 2) * 4 + x)


def send_groups():
    halves = len(SENDS)
    slots = len(SLOTS)
    columns = {(slot, piece) for slot, piece, _ in STEPS}
    pieces = len(columns)
    single_rows = len({dst for _, dst, _, _ in SENDS}) + len({slot for slot, _ in columns}) + 2 * slots - 1
    groups = []
    for count, each in ((pieces, 2 * PIECES), (single_rows, 2), (halves, 4 * PIECES)):
        sizes = []
        while count >= each:
            sizes.append(min(count // each, slots) * each)
            count -= sizes[-1]
        groups.append(sizes + [1] * count)
    return groups


def kernel(
    x_ref, id_ref, o_ref, x_in, id_in, rows, ids, id_rows, row_best, col_best, partial, returned,
    load_sem, sent, sent_small, sent_half, recv_sem, id_recv, twin_recv, twin_id_recv, home_recv,
):
    core = lax.axis_index("col")
    twin = 1 - core
    here = (0, 0, 0)
    neighbours = [device_at(direction, core) for direction in DIRECTIONS]
    other_core = device_at(here, twin)
    slots = len(SLOTS)

    barrier = pltpu.get_barrier_semaphore()
    for device in neighbours + [other_core]:
        pl.semaphore_signal(barrier, inc=1, device_id=device, device_id_type=MESH)
    load = pltpu.make_async_copy(x_ref, x_in, load_sem.at[0])
    load_ids = pltpu.make_async_copy(id_ref, id_in, load_sem.at[1])
    load.start()
    load_ids.start()

    def remote(src, dst, send, recv, device):
        return pltpu.make_async_remote_copy(
            src_ref=src, dst_ref=dst, send_sem=send, recv_sem=recv, device_id=device, device_id_type=MESH
        )

    def spread_ids(slot):
        for piece in range(PIECES):
            lane_ids = ids[slot, core, :, piece * PIECE:(piece + 1) * PIECE]
            id_rows[slot, piece] = jnp.broadcast_to(lane_ids, (PIECE, PIECE)).T

    piece_groups, row_groups, half_groups = send_groups()
    piece_sems = iter([sent.at[g] for g, size in enumerate(piece_groups) for _ in range(size)])
    half_sems = iter([sent_half.at[g] for g, size in enumerate(half_groups) for _ in range(size)])
    row_sems = iter([sent_small.at[g] for g, size in enumerate(row_groups) for _ in range(size)])

    def to_twin(slot, piece):
        copy = remote(
            rows.at[slot, piece, core], rows.at[slot, piece, core],
            next(piece_sems), twin_recv.at[slot, piece], other_core,
        )
        copy.start()

    def ids_to_twin(slot):
        copy = remote(
            ids.at[slot, core], ids.at[slot, core], next(row_sems), twin_id_recv.at[slot],
            other_core,
        )
        copy.start()

    def twin_wait(slot, piece):
        remote(
            rows.at[slot, piece, twin], rows.at[slot, piece, twin],
            sent.at[0], twin_recv.at[slot, piece], other_core,
        ).wait_recv()

    def twin_ids_wait(slot):
        remote(
            ids.at[slot, twin], ids.at[slot, twin], sent_small.at[0], twin_id_recv.at[slot],
            other_core,
        ).wait_recv()

    load_ids.wait()
    ids[0, core] = id_in[...].astype(jnp.float32)
    load.wait()
    features = x_in.shape[1]
    for piece in range(PIECES):
        values = x_in[piece * PIECE:(piece + 1) * PIECE].astype(jnp.float32)
        mean = jnp.mean(values * values, axis=-1, keepdims=True)
        scale = lax.rsqrt(mean + 1e-06) * (1.0 / features**0.5)
        rows[0, piece, core] = (values * scale).astype(jnp.bfloat16)
    pl.semaphore_wait(barrier, len(DIRECTIONS) + 1)

    twin_id_fresh = set()
    row_touched, col_touched, spread = set(), set(), set()

    def half_copy(index, semaphore):
        src, dst, half, direction = SENDS[index]
        place = pl.ds(half % 2 * (PIECE // 2), PIECE // 2)
        return remote(
            rows.at[src, half // 2, core, place], rows.at[dst, half // 2, core, place],
            semaphore, recv_sem.at[dst, half], neighbours[direction],
        )

    def id_copy(index, semaphore):
        src, dst, half, direction = SENDS[index]
        return remote(
            ids.at[src, core], ids.at[dst, core], semaphore, id_recv.at[dst],
            neighbours[direction],
        )

    as_columns = {(slot, piece) for slot, piece, _ in STEPS}
    have = set()
    for_twin = [(0, piece) for piece in range(PIECES)] + [(0, None)]

    def serve_twin():
        while for_twin:
            slot, piece = for_twin.pop(0)
            if piece is None:
                ids_to_twin(slot)
            else:
                to_twin(slot, piece)

    first_for = {}
    for kind, what in ORDER:
        if kind == 0:
            first_for.setdefault(SENDS[what][1], what)

    def arrive(index):
        src, dst, half, direction = SENDS[index]
        if first_for[dst] == index:
            id_copy(index, sent_small.at[0]).wait_recv()
            if dst in {slot for slot, _ in as_columns}:
                for_twin.append((dst, None))
        half_copy(index, sent.at[0]).wait_recv()
        have.add((dst, half))
        if (dst, half ^ 1) in have and (dst, half // 2) in as_columns:
            for_twin.append((dst, half // 2))

    def send(index):
        src, dst, half, direction = SENDS[index]
        half_copy(index, next(half_sems)).start()
        if first_for[dst] == index:
            id_copy(index, next(row_sems)).start()

    def step(work):
        batch, before, after = work
        for index in batch:
            slot, piece, _ = STEPS[index]
            if slot not in twin_id_fresh:
                twin_id_fresh.add(slot)
                twin_ids_wait(slot)
            twin_wait(slot, piece)

        @pl.when(core < 2)
        def _():
            for slot in before:
                sum_up(slot)
            for index in batch:
                compare(*STEPS[index])
            for slot in after:
                sum_up(slot)

        for slot in before + after:
            for to_core in range(2 if slot else 1):
                home_copy(slot, to_core).start()

    def compare(slot, piece, others):
        own = [(0, p) for p in range(PIECES)] if slot == 0 else []
        pieces = others + own
        for s in sorted({s for s, _ in pieces} - spread):
            spread.add(s)
            spread_ids(s)
        columns = rows[slot, piece].reshape(2 * PIECE, features)
        stacked = jnp.concatenate([rows[s, p, core] for s, p in pieces], axis=0)
        scores = lax.dot_general(stacked, columns, NT, preferred_element_type=jnp.float32)
        lane_ids = [ids[slot, half, :, piece * PIECE:(piece + 1) * PIECE] for half in range(2)]
        columns_best = [None, None]
        for at, (s, p) in enumerate(pieces):
            row = row_best[s, p] if (s, p) in row_touched else None
            row_touched.add((s, p))
            for half in range(2):
                block = scores[at * PIECE:(at + 1) * PIECE, half * PIECE:(half + 1) * PIECE]
                allowed = id_rows[s, p] == lane_ids[half]
                if s == slot and p == piece:
                    r = lax.broadcasted_iota(jnp.int32, (PIECE, PIECE), 0)
                    c = lax.broadcasted_iota(jnp.int32, (PIECE, PIECE), 1)
                    allowed = allowed & (r + PIECE * core != c + PIECE * half)
                block = jnp.where(allowed, block, NEG)
                row = block if row is None else jnp.maximum(row, block)
                if s != slot:
                    best = jnp.max(block.reshape(PIECE // 8, 8, PIECE), axis=0)
                    seen = columns_best[half]
                    columns_best[half] = best if seen is None else jnp.maximum(seen, best)
            row_best[s, p] = row
        if columns_best[0] is not None:
            for half in range(2):
                col_best[slot, piece, half] = columns_best[half]
            col_touched.add((slot, piece))

    def home_copy(slot, to_core):
        if slot == 0:
            target, semaphore, device = returned.at[0, core], home_recv.at[0], other_core
            return remote(partial.at[0, twin], target, next(row_sems), semaphore, device)
        target, semaphore, device = returned.at[slot, core], home_recv.at[1], device_at(SLOTS[slot], to_core)
        return remote(partial.at[slot, to_core], target, next(row_sems), semaphore, device)

    def sum_up(slot):
        for piece in range(PIECES):
            mine = None
            if (slot, piece) in row_touched:
                mine = jnp.max(row_best[slot, piece].T, axis=0, keepdims=True)
            for half in range(2):
                best = jnp.full((1, PIECE), NEG, jnp.float32)
                if mine is not None:
                    best = jnp.where(core == half, mine, best)
                if (slot, piece) in col_touched:
                    best = jnp.maximum(best, jnp.max(col_best[slot, piece, half], axis=0, keepdims=True))
                partial[slot, half, :, piece * PIECE:(piece + 1) * PIECE] = best

    for kind, what in ORDER:
        if kind != 1:
            serve_twin()
        (arrive, send, step)[kind](what)

    def arrived(array, semaphore):
        remote(array, array, sent.at[0], semaphore, other_core).wait_recv()

    def left(array, semaphore):
        remote(array, array, semaphore, home_recv.at[0], other_core).wait_send()

    returned[0, core] = partial[0, core]
    arrived(returned.at[0, twin], home_recv.at[0])
    arrived(returned.at[1:slots], home_recv.at[1])
    o_ref[...] = jnp.max(returned[...], axis=(0, 1))
    for group, size in enumerate(piece_groups):
        whole = size // (2 * PIECES)
        left(rows.at[0:whole] if whole else rows.at[0, 0, 0], sent.at[group])
    for group, size in enumerate(half_groups):
        whole = size // (4 * PIECES)
        left(rows.at[0:whole] if whole else rows.at[0, 0, 0, 0:PIECE // 2], sent_half.at[group])
    for group, size in enumerate(row_groups):
        whole = size // 2
        left(ids.at[0:whole] if whole else ids.at[0, 0], sent_small.at[group])


def local(embeddings, assignment):
    count, features = embeddings.shape
    slots = len(SLOTS)
    dma = pltpu.SemaphoreType.DMA
    piece_groups, row_groups, half_groups = send_groups()
    best = pl.pallas_call(
        kernel,
        out_shape=jax.ShapeDtypeStruct((1, count), jnp.float32),
        in_specs=[pl.BlockSpec(memory_space=pl.ANY)] * 2,
        out_specs=pl.BlockSpec(memory_space=pltpu.VMEM),
        scratch_shapes=[
            pltpu.VMEM((count, features), jnp.bfloat16),
            pltpu.VMEM((1, count), jnp.int32),
            pltpu.VMEM((slots, PIECES, 2, PIECE, features), jnp.bfloat16),
            pltpu.VMEM((slots, 2, 1, count), jnp.float32),
            pltpu.VMEM((slots, PIECES, PIECE, PIECE), jnp.float32),
            pltpu.VMEM((slots, PIECES, PIECE, PIECE), jnp.float32),
            pltpu.VMEM((slots, PIECES, 2, 8, PIECE), jnp.float32),
            pltpu.VMEM((slots, 2, 1, count), jnp.float32),
            pltpu.VMEM((slots, 2, 1, count), jnp.float32),
            dma((2,)),
            dma((len(piece_groups),)),
            dma((len(row_groups),)),
            dma((len(half_groups),)),
            dma((slots, 2 * PIECES)),
            dma((slots,)),
            dma((slots, PIECES)),
            dma((slots,)),
            dma((2,)),
        ],
        compiler_params=pltpu.CompilerParams(
            collective_id=0, has_side_effects=True, vmem_limit_bytes=56 * 2**20
        ),
    )(embeddings, assignment.reshape(1, count))
    return best.reshape(count)


def solution(mesh):
    axes = ("cluster", "col", "blk")
    return jax.shard_map(
        local, mesh=mesh, in_specs=(P(axes, None), P(axes, None)), out_specs=P(axes), check_vma=False
    )
```

```python
import jax
import jax.numpy as jnp
from jax import lax
from jax.experimental import pallas as pl
from jax.experimental.pallas import tpu as pltpu
from jax.sharding import PartitionSpec as P

MESH = pl.DeviceIdType.MESH
NT = (((1,), (1,)), ((), ()))
NEG = float("-inf")
PIECES = 3
PIECE = 128
DIRECTIONS = [(1, 0, 0), (-1, 0, 0), (0, 1, 0), (0, -1, 0), (0, 0, 1), (0, 0, -1)]
TWIST = 0
SLOTS = [
    (0, 0, 0), (0, 0, 1), (0, 0, 2), (0, 0, 3), (0, 1, 0), (0, 2, 0), (1, 0, 0), (1, 0, 2), (1, 0, 3), (1, 1, 3),
    (3, 0, 0), (3, 1, 0), (3, 2, 0), (3, 3, 0),
]
SENDS = [
    (0, 10, 4, 0), (0, 6, 2, 1), (0, 4, 2, 3), (0, 3, 4, 4), (0, 1, 0, 5), (0, 10, 5, 0), (0, 6, 3, 1), (0, 4, 3,
    3), (0, 3, 5, 4), (0, 1, 1, 5), (0, 10, 2, 0), (0, 6, 4, 1), (0, 4, 0, 3), (0, 3, 0, 4), (0, 1, 2, 5), (0, 10,
    3, 0), (0, 6, 5, 1), (0, 4, 1, 3), (0, 3, 1, 4), (0, 1, 3, 5), (0, 10, 0, 0), (0, 6, 0, 1), (0, 4, 4, 3), (0, 1,
    4, 5), (10, 13, 4, 2), (6, 8, 2, 4), (0, 10, 1, 0), (0, 6, 1, 1), (4, 5, 2, 3), (0, 1, 5, 5), (10, 13, 5, 2),
    (6, 8, 3, 4), (3, 8, 4, 1), (4, 5, 3, 3), (1, 2, 0, 5), (10, 13, 2, 2), (4, 11, 0, 0), (3, 8, 0, 1), (13, 12, 4,
    2), (4, 5, 0, 3), (1, 2, 2, 5), (10, 13, 3, 2), (6, 8, 5, 4), (4, 11, 1, 0), (3, 2, 1, 4), (3, 8, 1, 1), (13,
    12, 5, 2), (4, 5, 1, 3), (1, 2, 3, 5), (4, 11, 4, 0), (8, 7, 2, 4), (10, 13, 0, 2), (8, 9, 2, 3), (1, 2, 4, 5),
    (5, 12, 2, 0), (8, 7, 3, 4), (12, 5, 4, 1), (10, 13, 1, 2), (8, 9, 3, 3), (1, 2, 5, 5), (8, 7, 4, 4), (5, 12, 3,
    0), (2, 7, 0, 1), (11, 12, 0, 3), (8, 7, 5, 4), (2, 7, 1, 1), (2, 3, 2, 5), (12, 5, 5, 1), (12, 11, 5, 2), (11,
    12, 1, 3), (2, 3, 3, 5), (0, 4, 5, 3), (12, 11, 2, 2), (12, 11, 3, 2),
]
STEPS = [
    (0, 0, []),
    (0, 1, []),
    (0, 2, []),
    (10, 2, [(0, 0), (0, 1), (0, 2), (1, 0), (3, 2), (4, 1), (6, 1)]),
    (4, 1, [(0, 0), (0, 1), (0, 2), (1, 0), (3, 2), (6, 1)]),
    (6, 1, [(0, 0), (0, 1), (1, 0), (3, 2)]),
    (3, 2, [(0, 0), (0, 1), (0, 2), (1, 0), (1, 1), (4, 0), (6, 2), (10, 1)]),
    (1, 0, [(0, 0), (0, 1), (3, 0), (4, 0), (6, 2), (10, 1)]),
    (4, 0, [(0, 0), (0, 1), (0, 2), (1, 1), (3, 0), (6, 1), (6, 2), (10, 1), (10, 2), (13, 2)]),
    (3, 0, [(0, 1), (0, 2), (1, 1), (4, 1), (6, 1), (6, 2), (10, 1), (10, 2), (13, 2)]),
    (10, 1, [(0, 0), (0, 2), (1, 1), (4, 1), (6, 1)]),
    (6, 2, [(0, 0), (4, 1), (8, 1), (10, 0), (10, 2), (13, 2)]),
    (1, 1, [(0, 1), (4, 1), (6, 1), (8, 1), (13, 2)]),
    (13, 2, [(0, 2), (1, 0), (1, 2), (3, 2), (4, 1), (6, 0), (6, 1), (8, 1), (10, 2)]),
    (10, 0, [(0, 0), (1, 0), (3, 0), (4, 0), (4, 1), (5, 1), (6, 0), (6, 1), (8, 1), (8, 2)]),
    (8, 1, [(0, 2), (1, 0), (1, 2), (4, 0), (4, 1), (5, 1), (10, 1), (10, 2)]),
    (1, 2, [(3, 2), (4, 0), (4, 1), (5, 1), (8, 2), (10, 1)]),
    (6, 0, [(2, 0), (4, 0), (4, 1), (5, 1), (11, 0), (13, 1)]),
    (5, 1, [(0, 0), (0, 1), (0, 2), (1, 0), (1, 1), (2, 0), (3, 0), (3, 2), (6, 1), (6, 2), (8, 2), (13, 2)]),
    (8, 2, [(1, 0), (1, 1), (4, 0), (4, 1), (10, 1), (10, 2), (11, 0), (13, 1), (13, 2)]),
    (13, 1, [(0, 2), (1, 0), (1, 1), (1, 2), (2, 0), (2, 1), (3, 0), (3, 2), (6, 1), (6, 2), (8, 0), (8, 1), (10, 2)]),
    (11, 0, [(1, 0), (1, 1), (1, 2), (2, 0), (2, 1), (3, 0), (8, 0), (8, 1), (12, 2), (13, 2)]),
    (2, 0, [(4, 0), (4, 1), (5, 0), (10, 1), (10, 2), (12, 2), (13, 2)]),
    (12, 2, [(0, 2), (1, 0), (1, 1), (1, 2), (2, 1), (3, 0), (3, 2), (4, 0), (6, 0), (6, 1), (6, 2), (7, 1), (8, 0), (8, 1), (8, 2), (10, 2)]),
    (5, 0, [(0, 0), (1, 0), (1, 2), (3, 2), (6, 0), (6, 2), (7, 1), (8, 0), (8, 1), (8, 2)]),
    (8, 0, [(4, 1), (5, 1), (10, 0), (10, 1), (10, 2), (13, 2)]),
    (2, 1, [(0, 1), (4, 0), (4, 1), (5, 1), (12, 1), (13, 0), (13, 2)]),
    (7, 1, [(4, 1), (9, 1), (10, 0), (10, 1), (10, 2), (11, 0), (12, 1), (13, 0), (13, 1), (13, 2)]),
    (13, 0, [(0, 2), (1, 0), (1, 1), (1, 2), (2, 0), (2, 2), (3, 0), (3, 2), (6, 1), (6, 2), (7, 0), (7, 2), (8, 0), (8, 1), (8, 2), (9, 1)]),
    (12, 1, [(1, 0), (1, 1), (1, 2), (2, 0), (2, 2), (6, 0), (6, 1), (7, 0), (8, 0), (8, 1), (8, 2), (9, 1)]),
    (2, 2, [(4, 0), (4, 1), (5, 0), (5, 1), (5, 2), (11, 0), (11, 2), (12, 0), (12, 2), (13, 1), (13, 2)]),
    (11, 2, [(0, 2), (1, 0), (1, 1), (1, 2), (2, 0), (2, 1), (3, 0), (3, 1), (3, 2), (7, 1), (7, 2), (8, 0), (8, 1), (8, 2)]),
    (9, 1, [(0, 0), (0, 1), (0, 2)]),
    (7, 0, [(4, 1), (5, 0), (10, 0), (10, 2), (12, 0), (12, 2), (13, 2)]),
    (7, 2, [(4, 1), (10, 2), (12, 2)]),
    (12, 0, [(1, 0), (1, 1), (1, 2), (6, 0), (8, 0), (8, 2)]),
    (5, 2, [(1, 2), (8, 1)]),
    (3, 1, [(4, 0), (4, 2)]),
    (4, 2, [(1, 0), (1, 1), (1, 2), (2, 0), (2, 1), (2, 2), (3, 0), (3, 2)]),
    (11, 1, [(1, 0), (1, 1), (1, 2), (8, 0), (8, 2)]),
]
ORDER = [
    (1, 0),
    (1, 1),
    (1, 2),
    (1, 3),
    (1, 4),
    (1, 5),
    (1, 6),
    (1, 7),
    (1, 8),
    (1, 9),
    (1, 10),
    (1, 11),
    (1, 12),
    (1, 13),
    (1, 14),
    (2, ([0, 1, 2], [(9, 0), (9, 2)], [], [])),
    (1, 15),
    (1, 16),
    (1, 17),
    (1, 18),
    (1, 19),
    (1, 20),
    (1, 21),
    (1, 22),
    (1, 23),
    (0, 0),
    (1, 24),
    (0, 1),
    (1, 25),
    (0, 2),
    (0, 3),
    (0, 4),
    (1, 26),
    (1, 27),
    (1, 28),
    (1, 29),
    (0, 5),
    (1, 30),
    (0, 6),
    (1, 31),
    (0, 7),
    (0, 8),
    (0, 9),
    (1, 32),
    (1, 33),
    (1, 34),
    (0, 10),
    (1, 35),
    (0, 11),
    (0, 12),
    (1, 36),
    (0, 13),
    (0, 14),
    (2, ([3, 4, 5], [], [], [])),
    (0, 24),
    (1, 37),
    (1, 38),
    (1, 39),
    (1, 40),
    (0, 15),
    (1, 41),
    (0, 16),
    (1, 42),
    (0, 17),
    (1, 43),
    (0, 18),
    (1, 44),
    (0, 19),
    (2, ([6, 7], [], [], [])),
    (0, 30),
    (1, 45),
    (1, 46),
    (1, 47),
    (1, 48),
    (0, 20),
    (0, 21),
    (0, 22),
    (1, 49),
    (0, 25),
    (1, 50),
    (0, 23),
    (2, ([8, 9, 10], [], [], [])),
    (0, 35),
    (1, 51),
    (1, 52),
    (1, 53),
    (0, 26),
    (0, 27),
    (0, 28),
    (1, 54),
    (0, 31),
    (1, 55),
    (0, 29),
    (2, ([11, 12, 13], [], [], [])),
    (0, 38),
    (1, 56),
    (1, 57),
    (1, 58),
    (1, 59),
    (0, 36),
    (0, 32),
    (1, 60),
    (0, 33),
    (1, 61),
    (0, 42),
    (0, 34),
    (1, 62),
    (2, ([14, 15, 16], [], [], [])),
    (0, 41),
    (1, 63),
    (1, 64),
    (0, 43),
    (0, 37),
    (0, 39),
    (0, 44),
    (1, 65),
    (0, 40),
    (1, 66),
    (2, ([17, 18, 19], [], [], [])),
    (0, 46),
    (1, 67),
    (1, 68),
    (1, 69),
    (0, 49),
    (0, 45),
    (0, 47),
    (0, 50),
    (0, 48),
    (1, 70),
    (2, ([20, 21, 22], [], [], [])),
    (0, 51),
    (1, 71),
    (0, 54),
    (1, 72),
    (0, 56),
    (0, 52),
    (0, 55),
    (0, 53),
    (2, ([23, 24, 25], [], [], [])),
    (0, 57),
    (0, 61),
    (1, 73),
    (0, 62),
    (0, 58),
    (0, 60),
    (0, 59),
    (2, ([26, 27], [], [], [])),
    (0, 68),
    (0, 65),
    (0, 63),
    (0, 64),
    (0, 66),
    (2, ([28, 29], [(10, 1)], [], [])),
    (0, 67),
    (0, 69),
    (0, 70),
    (0, 72),
    (2, ([30, 31, 32], [(6, 1), (6, 2), (12, 1), (13, 0)], [], [])),
    (0, 71),
    (0, 73),
    (2, ([33, 34, 35], [(0, 0), (0, 1), (0, 2), (5, 1), (7, 1), (9, 1), (11, 0), (11, 2), (13, 1)], [], [9, 0])),
    (2, ([36, 37], [(4, 1), (5, 0), (6, 0), (7, 0), (7, 2), (10, 0), (10, 2), (12, 0), (12, 2), (13, 2)], [], [7, 12, 13, 6, 10])),
    (2, ([38, 39], [(3, 1), (4, 0), (5, 2), (8, 1)], [(1, 0), (1, 1), (1, 2), (2, 0), (2, 1), (2, 2), (3, 0), (3, 2), (4, 2), (8, 0), (8, 2), (11, 1)], [5, 2, 8, 11, 1, 3, 4])),
]


def device_at(offset, core):
    cluster = lax.axis_index("cluster")
    blk = lax.axis_index("blk")
    x, y, z = blk % 4, cluster // 2, (cluster % 2) * 2 + blk // 4
    odd = z % 2
    dx, dy, dz = offset
    if TWIST == 1:
        dx, dy = dx - odd * (dx + dy), dy - odd * (dx + dy)
    elif TWIST == 2:
        dx, dy = dx + odd * (dy - dx), dy + odd * (dx - dy)
    elif TWIST == 3:
        dx, dy = dx - odd * (2 * dx), dy - odd * (2 * dy)
    elif TWIST == 4:
        dx = dx - odd * (2 * dx)
    x, y, z = (x + dx + 8) % 4, (y + dy + 8) % 4, (z + dz + 8) % 4
    return (y * 2 + z // 2, core, (z % 2) * 4 + x)


def send_groups():
    halves = len(SENDS)
    slots = len(SLOTS)
    columns = {(slot, piece) for slot, piece, _ in STEPS}
    pieces = len(columns)
    single_rows = len({dst for _, dst, _, _ in SENDS}) + len({slot for slot, _ in columns}) + 2 * slots - 1
    groups = []
    for count, each in ((pieces, 2 * PIECES), (single_rows, 2), (halves, 4 * PIECES)):
        sizes = []
        while count >= each:
            sizes.append(min(count // each, slots) * each)
            count -= sizes[-1]
        groups.append(sizes + [1] * count)
    return groups


def kernel(
    x_ref, id_ref, o_ref, x_in, id_in, rows, ids, id_rows, row_best, col_best, partial, returned,
    load_sem, sent, sent_small, sent_half, recv_sem, id_recv, twin_recv, twin_id_recv, home_recv,
):
    core = lax.axis_index("col")
    twin = 1 - core
    here = (0, 0, 0)
    neighbours = [device_at(direction, core) for direction in DIRECTIONS]
    other_core = device_at(here, twin)
    slots = len(SLOTS)

    barrier = pltpu.get_barrier_semaphore()
    for device in neighbours + [other_core]:
        pl.semaphore_signal(barrier, inc=1, device_id=device, device_id_type=MESH)
    load = pltpu.make_async_copy(x_ref, x_in, load_sem.at[0])
    load_ids = pltpu.make_async_copy(id_ref, id_in, load_sem.at[1])
    load.start()
    load_ids.start()

    def remote(src, dst, send, recv, device):
        return pltpu.make_async_remote_copy(
            src_ref=src, dst_ref=dst, send_sem=send, recv_sem=recv, device_id=device, device_id_type=MESH
        )

    def spread_ids(slot):
        for piece in range(PIECES):
            lane_ids = ids[slot, core, :, piece * PIECE:(piece + 1) * PIECE]
            id_rows[slot, piece] = jnp.broadcast_to(lane_ids, (PIECE, PIECE)).T

    piece_groups, row_groups, half_groups = send_groups()
    piece_sems = iter([sent.at[g] for g, size in enumerate(piece_groups) for _ in range(size)])
    half_sems = iter([sent_half.at[g] for g, size in enumerate(half_groups) for _ in range(size)])
    row_sems = iter([sent_small.at[g] for g, size in enumerate(row_groups) for _ in range(size)])

    def to_twin(slot, piece):
        copy = remote(
            rows.at[slot, piece, core], rows.at[slot, piece, core],
            next(piece_sems), twin_recv.at[slot, piece], other_core,
        )
        copy.start()

    def ids_to_twin(slot):
        copy = remote(
            ids.at[slot, core], ids.at[slot, core], next(row_sems), twin_id_recv.at[slot],
            other_core,
        )
        copy.start()

    def twin_wait(slot, piece):
        remote(
            rows.at[slot, piece, twin], rows.at[slot, piece, twin],
            sent.at[0], twin_recv.at[slot, piece], other_core,
        ).wait_recv()

    def twin_ids_wait(slot):
        remote(
            ids.at[slot, twin], ids.at[slot, twin], sent_small.at[0], twin_id_recv.at[slot],
            other_core,
        ).wait_recv()

    load_ids.wait()
    ids[0, core] = id_in[...].astype(jnp.float32)
    load.wait()
    features = x_in.shape[1]
    for piece in range(PIECES):
        values = x_in[piece * PIECE:(piece + 1) * PIECE].astype(jnp.float32)
        mean = jnp.mean(values * values, axis=-1, keepdims=True)
        scale = lax.rsqrt(mean + 1e-06) * (1.0 / features**0.5)
        rows[0, piece, core] = (values * scale).astype(jnp.bfloat16)
    pl.semaphore_wait(barrier, len(DIRECTIONS) + 1)

    twin_id_fresh = set()
    row_touched, col_touched, spread = set(), set(), set()

    def half_copy(index, semaphore):
        src, dst, half, direction = SENDS[index]
        place = pl.ds(half % 2 * (PIECE // 2), PIECE // 2)
        return remote(
            rows.at[src, half // 2, core, place], rows.at[dst, half // 2, core, place],
            semaphore, recv_sem.at[dst, half], neighbours[direction],
        )

    def id_copy(index, semaphore):
        src, dst, half, direction = SENDS[index]
        return remote(
            ids.at[src, core], ids.at[dst, core], semaphore, id_recv.at[dst],
            neighbours[direction],
        )

    as_columns = {(slot, piece) for slot, piece, _ in STEPS}
    have = set()
    for_twin = [(0, piece) for piece in range(PIECES)] + [(0, None)]

    def serve_twin():
        while for_twin:
            slot, piece = for_twin.pop(0)
            if piece is None:
                ids_to_twin(slot)
            else:
                to_twin(slot, piece)

    first_for = {}
    for kind, what in ORDER:
        if kind == 0:
            first_for.setdefault(SENDS[what][1], what)

    def arrive(index):
        src, dst, half, direction = SENDS[index]
        if first_for[dst] == index:
            id_copy(index, sent_small.at[0]).wait_recv()
            if dst in {slot for slot, _ in as_columns}:
                for_twin.append((dst, None))
        half_copy(index, sent.at[0]).wait_recv()
        have.add((dst, half))
        if (dst, half ^ 1) in have and (dst, half // 2) in as_columns:
            for_twin.append((dst, half // 2))

    def send(index):
        src, dst, half, direction = SENDS[index]
        half_copy(index, next(half_sems)).start()
        if first_for[dst] == index:
            id_copy(index, next(row_sems)).start()

    def step(work):
        batch, before, after, complete = work
        for index in batch:
            slot, piece, _ = STEPS[index]
            if slot not in twin_id_fresh:
                twin_id_fresh.add(slot)
                twin_ids_wait(slot)
            twin_wait(slot, piece)

        @pl.when(core < 2)
        def _():
            for slot, piece in before:
                sum_up(slot, piece)
            for index in batch:
                compare(*STEPS[index])
            for slot, piece in after:
                sum_up(slot, piece)

        for slot in complete:
            for to_core in range(2 if slot else 1):
                home_copy(slot, to_core).start()

    def compare(slot, piece, others):
        own = [(0, p) for p in range(PIECES)] if slot == 0 else []
        pieces = others + own
        for s in sorted({s for s, _ in pieces} - spread):
            spread.add(s)
            spread_ids(s)
        columns = rows[slot, piece].reshape(2 * PIECE, features)
        stacked = jnp.concatenate([rows[s, p, core] for s, p in pieces], axis=0)
        scores = lax.dot_general(stacked, columns, NT, preferred_element_type=jnp.float32)
        lane_ids = [ids[slot, half, :, piece * PIECE:(piece + 1) * PIECE] for half in range(2)]
        columns_best = [None, None]
        for at, (s, p) in enumerate(pieces):
            row = row_best[s, p] if (s, p) in row_touched else None
            row_touched.add((s, p))
            for half in range(2):
                block = scores[at * PIECE:(at + 1) * PIECE, half * PIECE:(half + 1) * PIECE]
                allowed = id_rows[s, p] == lane_ids[half]
                if s == slot and p == piece:
                    r = lax.broadcasted_iota(jnp.int32, (PIECE, PIECE), 0)
                    c = lax.broadcasted_iota(jnp.int32, (PIECE, PIECE), 1)
                    allowed = allowed & (r + PIECE * core != c + PIECE * half)
                block = jnp.where(allowed, block, NEG)
                row = block if row is None else jnp.maximum(row, block)
                if s != slot:
                    best = jnp.max(block.reshape(PIECE // 8, 8, PIECE), axis=0)
                    seen = columns_best[half]
                    columns_best[half] = best if seen is None else jnp.maximum(seen, best)
            row_best[s, p] = row
        if columns_best[0] is not None:
            for half in range(2):
                col_best[slot, piece, half] = columns_best[half]
            col_touched.add((slot, piece))

    def home_copy(slot, to_core):
        if slot == 0:
            target, semaphore, device = returned.at[0, core], home_recv.at[0], other_core
            return remote(partial.at[0, twin], target, next(row_sems), semaphore, device)
        target, semaphore, device = returned.at[slot, core], home_recv.at[1], device_at(SLOTS[slot], to_core)
        return remote(partial.at[slot, to_core], target, next(row_sems), semaphore, device)

    def sum_up(slot, piece):
        mine = None
        if (slot, piece) in row_touched:
            mine = jnp.max(row_best[slot, piece].T, axis=0, keepdims=True)
        for half in range(2):
            best = jnp.full((1, PIECE), NEG, jnp.float32)
            if mine is not None:
                best = jnp.where(core == half, mine, best)
            if (slot, piece) in col_touched:
                best = jnp.maximum(best, jnp.max(col_best[slot, piece, half], axis=0, keepdims=True))
            partial[slot, half, :, piece * PIECE:(piece + 1) * PIECE] = best

    for kind, what in ORDER:
        if kind != 1:
            serve_twin()
        (arrive, send, step)[kind](what)

    def arrived(array, semaphore):
        remote(array, array, sent.at[0], semaphore, other_core).wait_recv()

    def left(array, semaphore):
        remote(array, array, semaphore, home_recv.at[0], other_core).wait_send()

    returned[0, core] = partial[0, core]
    arrived(returned.at[0, twin], home_recv.at[0])
    arrived(returned.at[1:slots], home_recv.at[1])
    o_ref[...] = jnp.max(returned[...], axis=(0, 1))
    for group, size in enumerate(piece_groups):
        whole = size // (2 * PIECES)
        left(rows.at[0:whole] if whole else rows.at[0, 0, 0], sent.at[group])
    for group, size in enumerate(half_groups):
        whole = size // (4 * PIECES)
        left(rows.at[0:whole] if whole else rows.at[0, 0, 0, 0:PIECE // 2], sent_half.at[group])
    for group, size in enumerate(row_groups):
        whole = size // 2
        left(ids.at[0:whole] if whole else ids.at[0, 0], sent_small.at[group])


def local(embeddings, assignment):
    count, features = embeddings.shape
    slots = len(SLOTS)
    dma = pltpu.SemaphoreType.DMA
    piece_groups, row_groups, half_groups = send_groups()
    best = pl.pallas_call(
        kernel,
        out_shape=jax.ShapeDtypeStruct((1, count), jnp.float32),
        in_specs=[pl.BlockSpec(memory_space=pl.ANY)] * 2,
        out_specs=pl.BlockSpec(memory_space=pltpu.VMEM),
        scratch_shapes=[
            pltpu.VMEM((count, features), jnp.bfloat16),
            pltpu.VMEM((1, count), jnp.int32),
            pltpu.VMEM((slots, PIECES, 2, PIECE, features), jnp.bfloat16),
            pltpu.VMEM((slots, 2, 1, count), jnp.float32),
            pltpu.VMEM((slots, PIECES, PIECE, PIECE), jnp.float32),
            pltpu.VMEM((slots, PIECES, PIECE, PIECE), jnp.float32),
            pltpu.VMEM((slots, PIECES, 2, 8, PIECE), jnp.float32),
            pltpu.VMEM((slots, 2, 1, count), jnp.float32),
            pltpu.VMEM((slots, 2, 1, count), jnp.float32),
            dma((2,)),
            dma((len(piece_groups),)),
            dma((len(row_groups),)),
            dma((len(half_groups),)),
            dma((slots, 2 * PIECES)),
            dma((slots,)),
            dma((slots, PIECES)),
            dma((slots,)),
            dma((2,)),
        ],
        compiler_params=pltpu.CompilerParams(
            collective_id=0, has_side_effects=True, vmem_limit_bytes=56 * 2**20
        ),
    )(embeddings, assignment.reshape(1, count))
    return best.reshape(count)


def solution(mesh):
    axes = ("cluster", "col", "blk")
    return jax.shard_map(
        local, mesh=mesh, in_specs=(P(axes, None), P(axes, None)), out_specs=P(axes), check_vma=False
    )
```
